256 devices in a mesh: expert: 32 (over y, x, core), tensor: 8 (over z).
Axes of the slice: x: 4, y: 4, z: 8, core: 2. Of those that a mesh axis runs over, the one named last changes fastest.
Arguments:
- tokens: bfloat16 [4096, 3584], P('expert', 'tensor'), may hold values from -6 to 6
- cotangent: bfloat16 [4096, 3584], P('expert', 'tensor'), may hold values from -3 to 3
- routes: int32 [4096, 2], P('expert'), may hold values from 0 to 15, all different within a row; in each aligned block of 128 rows (0 to 127, 128 to 255, ...) at most 20 rows name the same one
- route_weights: float32 [4096, 2], P('expert'), may hold values from 0.1 to 1
- dense_gate: bfloat16 [8, 608, 3584], P('tensor', 'expert'), may hold values from -0.09375 to 0.09375
- dense_up: bfloat16 [8, 608, 3584], P('tensor', 'expert'), may hold values from -0.09375 to 0.09375
- dense_down: bfloat16 [8, 608, 3584], P('tensor', 'expert'), may hold values from -0.078125 to 0.078125
- expert_gate: bfloat16 [38912, 3584], P(('expert', 'tensor')), may hold values from -0.09375 to 0.09375
- expert_up: bfloat16 [38912, 3584], P(('expert', 'tensor')), may hold values from -0.09375 to 0.09375
- expert_down: bfloat16 [38912, 3584], P(('expert', 'tensor')), may hold values from -0.125 to 0.125
Outputs:
- grad_input: bfloat16 [4096, 3584], P('expert', 'tensor')
- grad_expert_gate: bfloat16 [38912, 3584], P(('expert', 'tensor'))
- grad_expert_up: bfloat16 [38912, 3584], P(('expert', 'tensor'))
- grad_expert_down: bfloat16 [38912, 3584], P(('expert', 'tensor'))
The draws below stay inside these ranges and needn't reach their ends.
Inputs may be any that keep to these rules, and one draw needn't show every extreme that they name: `routes`: among the tokens of one owner (aligned blocks of 128 tokens) each expert is named at most 20 times; a token names 2 different experts.
All inputs are finite; a program needn't handle non-finite values.
Results may differ from the reference program's by a relative error of at most 0.019.
Values may be sent and summed in bfloat16 or wider, within the bound.
A program may use at most 256 MiB of HBM per device.

```python
import math
import jax
import jax.numpy as jnp
import numpy as np
from jax import lax

D = 3584
FF = 4864
FE = 2432
TOP = 2
GROUP = 2
TOK_DEV = 128
TOKENS = 4096
EXPERTS = 16
CAP = 20
FF_BLOCK = 608
FE_BLOCK = 152
N_EXPERT = 32
N_TENSOR = 8


def steps_of(rng, shape, shards, least, high):
    loudness, own = 1.0, jax.random.fold_in(rng, 6)
    for axis_at, blocks in shards:
        draws = jnp.exp(jax.random.uniform(jax.random.fold_in(own, axis_at), (blocks,), jnp.float32, least / len(shards), high / len(shards)))
        loudness = loudness * jnp.repeat(draws, shape[axis_at] // blocks).reshape([-1 if axis == axis_at else 1 for axis in range(len(shape))])
    return loudness


def deal_out(stream_key, own, number, rows, number_of, top, bound, skew):
    ranking = jax.random.permutation(stream_key, number_of)
    crowded, ordinary = portions_of(number_of, rows * top, bound, skew, True), portions_of(number_of, rows * top, bound, skew, False)
    places = jnp.arange(number_of)

    def named(tallies, rotation):
        used = int((tallies > 0).sum())
        fixed = max(1, used // 4)
        shifted = fixed + (places - fixed + rotation * (used - fixed)) % max(1, number_of - fixed)
        return jnp.zeros((number_of,), jnp.int32).at[ranking[jnp.where(places < fixed, places, shifted)]].set(jnp.asarray(tallies, jnp.int32))

    tallies = jnp.where(number % 4 == 0, named(crowded, number // 4), named(ordinary, number - number // 4 - 1))
    mixed = jax.random.permutation(jax.random.fold_in(own, 3), number_of)
    source_of, taker = mixed[0:number_of // 2 * 2:2], mixed[1:number_of // 2 * 2:2]
    margin = jnp.minimum(tallies[source_of] - 1, bound - tallies[taker]) // 2
    margin = jnp.where((source_of == ranking[0]) | (taker == ranking[0]) | (tallies[taker] == 0), 0, jnp.maximum(margin, 0))
    shifted = jax.random.randint(jax.random.fold_in(own, 4), (number_of // 2,), 0, 1 << 20) % (margin + 1)
    tallies = tallies.at[source_of].add(-shifted).at[taker].add(shifted)
    members = jnp.searchsorted(jnp.cumsum(tallies), jnp.arange(rows * top), side="right").astype(jnp.int32)
    listing = members.reshape(top, rows).T
    listing = listing[jax.random.permutation(jax.random.fold_in(own, 1), rows)]
    rotation = jax.random.randint(jax.random.fold_in(own, 2), (rows, 1), 0, top)
    return jnp.take_along_axis(listing, (jnp.arange(top)[None, :] + rotation) % top, axis=1)


def portions_of(count, total, most, skew, full):
    weights = [(1 << 20) // math.isqrt(grade ** skew) + 1 for grade in range(1, count + 1)]
    largest = most if full else min(most, max(-(-total // count), total * weights[0] // sum(weights)))
    least = 1 if total - largest >= count - 1 else 0
    holding, rest = [largest] + [least] * (count - 1), total - largest - least * (count - 1)
    while rest > 0:
        free = [i for i in range(1, count) if holding[i] < largest] or [i for i in range(1, count) if holding[i] < most]
        pool, left = sum([weights[i] for i in free]), rest
        for i in free:
            extra = min(most - holding[i], max(1, left * weights[i] // pool), rest)
            holding[i] = holding[i] + extra
            rest = rest - extra
    return np.array(holding)


def noise(stream_key, dims, deviation, reach, cuts=(), held_as=jnp.bfloat16):
    factor_of = steps_of(stream_key, dims, cuts, -0.22, 0.18) if cuts else 1.0
    entries = jax.random.normal(stream_key, dims, jnp.float32) * deviation * factor_of
    return jnp.minimum(jnp.maximum(entries, -reach), reach).astype(held_as)


def setup_inputs(seed: int = 0) -> dict:
    key_list = jax.random.split(jax.random.key(seed), 11)
    tokens = noise(key_list[0], (TOKENS, D), 1.0, 6.0, ((0, 32), (1, 8)))
    cotangent = noise(key_list[1], (TOKENS, D), 0.5, 3.0, ((0, 32), (1, 8)))
    routes_keys = jax.random.split(jax.random.fold_in(key_list[2], 1), TOKENS // TOK_DEV)
    routes_turns = jax.random.permutation(jax.random.fold_in(key_list[2], 3), TOKENS // TOK_DEV)
    routes = jax.vmap(lambda own, number: deal_out(jax.random.fold_in(key_list[2], 2), own, number, TOK_DEV, EXPERTS, TOP, CAP, 2))(routes_keys, routes_turns).reshape((TOKENS, TOP))
    route_weights = jnp.clip(jnp.exp(math.log(1.0) - 2.3025851 * jax.random.uniform(key_list[3], (TOKENS, TOP), jnp.float32) ** steps_of(key_list[3], (TOKENS, TOP), ((0, 32),), -0.2, 0.2)), 0.1, 1.0)
    dense_gate = noise(key_list[4], (N_TENSOR, FF_BLOCK, D), D ** -0.5, 0.09375, ((0, 8), (1, 32)))
    dense_up = noise(key_list[5], (N_TENSOR, FF_BLOCK, D), D ** -0.5, 0.09375, ((0, 8), (1, 32)))
    dense_down = noise(key_list[6], (N_TENSOR, FF_BLOCK, D), FF ** -0.5, 0.078125, ((0, 8), (1, 32)))
    expert_gate = noise(key_list[7], (EXPERTS * FE, D), D ** -0.5, 0.09375, ((0, 256),))
    expert_up = noise(key_list[8], (EXPERTS * FE, D), D ** -0.5, 0.09375, ((0, 256),))
    expert_down = noise(key_list[9], (EXPERTS * FE, D), FE ** -0.5, 0.125, ((0, 256),))
    return dict(tokens=tokens, cotangent=cotangent, routes=routes, route_weights=route_weights, dense_gate=dense_gate, dense_up=dense_up, dense_down=dense_down, expert_gate=expert_gate, expert_up=expert_up, expert_down=expert_down)


def dot_rows(left, right):
    return lax.dot_general(left, right, (((1,), (1,)), ((), ())), preferred_element_type=jnp.float32)


def dot_cols(left, right):
    return lax.dot_general(left, right, (((0,), (0,)), ((), ())), preferred_element_type=jnp.float32)


def rounded(value):
    narrow = value.astype(jnp.bfloat16)
    narrow = lax.optimization_barrier(narrow)
    return narrow.astype(jnp.float32)


def swiglu_grads(gate_pre, up_pre, grad_hidden):
    sigmoid_gate = jax.nn.sigmoid(gate_pre)
    silu_gate = gate_pre * sigmoid_gate
    slopes = sigmoid_gate * (1.0 + gate_pre * (1.0 - sigmoid_gate))
    grad_gate = (grad_hidden * up_pre * slopes).astype(jnp.bfloat16)
    grad_up = (grad_hidden * silu_gate).astype(jnp.bfloat16)
    return silu_gate, grad_gate, grad_up


def slot_ranks(flat_ids, count):
    onehot = (flat_ids[:, None] == jnp.arange(count, dtype=jnp.int32)[None, :]).astype(jnp.int32)
    before = jnp.cumsum(onehot, axis=0) - onehot
    return jnp.sum(before * onehot, axis=1).astype(jnp.int32)


def reference(tokens, cotangent, routes, route_weights, dense_gate, dense_up, dense_down, expert_gate, expert_up, expert_down):
    gate_flat = dense_gate.reshape(FF, D)
    up_flat = dense_up.reshape(FF, D)
    down_flat = dense_down.reshape(FF, D)
    gate_pre = dot_rows(tokens, gate_flat)
    up_pre = dot_rows(tokens, up_flat)
    grad_hidden = dot_rows(cotangent, down_flat)
    silu_gate, grad_gate, grad_up = swiglu_grads(gate_pre, up_pre, grad_hidden)
    dense_in = jnp.zeros((TOKENS, D), jnp.float32)
    for block_idx in range(N_TENSOR):
        lower = block_idx * FF_BLOCK
        upper = lower + FF_BLOCK
        term = jnp.dot(grad_gate[:, lower:upper], gate_flat[lower:upper], preferred_element_type=jnp.float32) + jnp.dot(grad_up[:, lower:upper], up_flat[lower:upper], preferred_element_type=jnp.float32)
        dense_in = dense_in + rounded(term)
    flat_ids = routes.reshape(-1).astype(jnp.int32)
    ranks = jax.vmap(lambda owner_ids: slot_ranks(owner_ids, EXPERTS))(routes.reshape(N_EXPERT, TOK_DEV * TOP)).reshape(-1)
    owners = jnp.arange(TOKENS * TOP, dtype=jnp.int32) // (TOK_DEV * TOP)
    slots = (owners * CAP + ranks).astype(jnp.int32)
    copies = jnp.repeat(tokens, TOP, axis=0)
    weighted = (jnp.repeat(cotangent, TOP, axis=0).astype(jnp.float32) * route_weights.reshape(-1)[:, None]).astype(jnp.bfloat16)
    slot_tokens = jnp.zeros((EXPERTS, N_EXPERT * CAP, D), jnp.bfloat16).at[flat_ids, slots].set(copies)
    slot_cot = jnp.zeros((EXPERTS, N_EXPERT * CAP, D), jnp.bfloat16).at[flat_ids, slots].set(weighted)
    gate_all = expert_gate.reshape(EXPERTS, FE, D)
    up_all = expert_up.reshape(EXPERTS, FE, D)
    down_all = expert_down.reshape(EXPERTS, FE, D)

    def one_expert(operands):
        rows_in, rows_cot, weight_gate, weight_up, weight_down = operands
        pre_gate = dot_rows(rows_in, weight_gate)
        pre_up = dot_rows(rows_in, weight_up)
        hidden_grad = dot_rows(rows_cot, weight_down)
        silu_pre, expert_grad_gate, expert_grad_up = swiglu_grads(pre_gate, pre_up, hidden_grad)
        hidden = (silu_pre * pre_up).astype(jnp.bfloat16)
        grad_down = dot_cols(hidden, rows_cot).astype(jnp.bfloat16)
        grad_gate_w = dot_cols(expert_grad_gate, rows_in).astype(jnp.bfloat16)
        grad_up_w = dot_cols(expert_grad_up, rows_in).astype(jnp.bfloat16)

        def add_block(block_idx, total):
            lower = (block_idx * FE_BLOCK).astype(jnp.int32)
            part_gate = lax.dynamic_slice_in_dim(expert_grad_gate, lower, FE_BLOCK, 1)
            part_up = lax.dynamic_slice_in_dim(expert_grad_up, lower, FE_BLOCK, 1)
            rows_gate = lax.dynamic_slice_in_dim(weight_gate, lower, FE_BLOCK, 0)
            rows_up = lax.dynamic_slice_in_dim(weight_up, lower, FE_BLOCK, 0)
            term = jnp.dot(part_gate, rows_gate, preferred_element_type=jnp.float32) + jnp.dot(part_up, rows_up, preferred_element_type=jnp.float32)
            return total + rounded(term)

        slot_in = lax.fori_loop(0, GROUP * N_TENSOR, add_block, jnp.zeros((N_EXPERT * CAP, D), jnp.float32))
        return grad_gate_w, grad_up_w, grad_down, slot_in

    grads_gate, grads_up, grads_down, slot_in = lax.map(one_expert, (slot_tokens, slot_cot, gate_all, up_all, down_all))
    expert_in = slot_in[flat_ids, slots].reshape(TOKENS, TOP, D).sum(axis=1)
    grad_input = (dense_in + expert_in).astype(jnp.bfloat16)
    grad_expert_gate = grads_gate.reshape(EXPERTS * FE, D)
    grad_expert_up = grads_up.reshape(EXPERTS * FE, D)
    grad_expert_down = grads_down.reshape(EXPERTS * FE, D)
    return (grad_input, grad_expert_gate, grad_expert_up, grad_expert_down)
```

```python
import jax
import jax.numpy as jnp
from jax import lax
from jax.experimental import pallas as pl
from jax.experimental.pallas import tpu as pltpu
from jax.sharding import PartitionSpec as P

MESH = pl.DeviceIdType.MESH
BF, F32 = jnp.bfloat16, jnp.float32
NT = (((1,), (1,)), ((), ()))
NN = (((1,), (0,)), ((), ()))
ROWS = 19
PAIR = 896
WIDE = 1152
BACK = 4480


def dot(a, b, dims=NN):
    return lax.dot_general(a, b, dims, preferred_element_type=F32)


def iota(shape, dim):
    return lax.broadcasted_iota(jnp.int32, shape, dim)


def onehot(mask):
    return jnp.where(mask, 1.0, 0.0).astype(BF)


def swiglu(gate, up, grad):
    sig = 1.0 / (1.0 + jnp.exp(-gate))
    silu = gate * sig
    slope = sig * (1.0 + gate * (1.0 - sig))
    return silu, (grad * up * slope).astype(BF), (grad * silu).astype(BF)


def kernel(
    mine, other, place_m, place_l, comb_m, comb_l, w_m, w_l, wblk, eg, eu, ed,
    out_x, out_g, out_u, out_d,
    got, packed, shards, lbuf, wall, sib_w, grm, grl, hm, hl, sib_m, sib_l,
    tr, lstack, fsend, frecv, xc, ggt, rs_send, rs_recv,
    p_sem, c_s, c_r, d_s, d_r, m_s, m_r, b_s, b_r, bm_s, bm_r, w_s, w_r,
    g_s, g_r, f_s, f_r, a_s, a_r, r_s, r_r, loc,
):
    i = lax.axis_index("expert")
    z = lax.axis_index("tensor")
    c = lax.rem(i, 2)
    j = lax.div(i, 2)
    y, x = lax.div(j, 4), lax.rem(j, 4)
    sib = i + 1 - 2 * c
    first = (1 - c) * x + c * y
    second = (1 - c) * y + c * x

    def plane(f, s):
        yy = (1 - c) * s + c * f
        xx = (1 - c) * f + c * s
        return ((yy * 4 + xx) * 2 + c, z)

    def shifted(v, s, n):
        return lax.rem(v + s + n, n)

    pending = []

    def send(src, dst, s_sem, r_sem, dev):
        copy = pltpu.make_async_remote_copy(
            src_ref=src, dst_ref=dst, send_sem=s_sem, recv_sem=r_sem,
            device_id=dev, device_id_type=MESH,
        )
        copy.start()
        pending.append(copy)

    def arrived(ref, s_sem, r_sem):
        pltpu.make_async_remote_copy(
            src_ref=ref, dst_ref=ref, send_sem=s_sem, recv_sem=r_sem,
            device_id=(sib, z), device_id_type=MESH,
        ).wait_recv()

    def chip(k):
        xx = lax.rem(x + k % 4, 4)
        yy = lax.rem(y + k // 4, 4)
        return yy * 4 + xx

    def chip_back(k):
        xx = lax.rem(x + 4 - k % 4, 4)
        yy = lax.rem(y + 4 - k // 4, 4)
        return yy * 4 + xx

    barrier = pltpu.get_barrier_semaphore()
    for k in range(1, 16):
        pl.semaphore_signal(barrier, inc=1, device_id=(chip(k) * 2 + c, z), device_id_type=MESH)
    pl.semaphore_signal(barrier, inc=1, device_id=(sib, z), device_id_type=MESH)
    for s in range(1, 8):
        pl.semaphore_signal(barrier, inc=1, device_id=(i, shifted(z, s, 8)), device_id_type=MESH)
    pl.semaphore_wait(barrier, 23)

    even = lax.rem(z, 2) == 0
    partner = z + 1 - 2 * lax.rem(z, 2)
    send(other, got, p_sem.at[0], p_sem.at[1], (i, partner))

    def block(pos, half=None):
        ref = wall.at[c, pos]
        return ref if half is None else ref.at[pl.ds(32 * half, 32), :]

    own_pos = second * 4 + first
    here = pltpu.make_async_copy(wblk, wall.at[c, own_pos], loc.at[0])
    here.start()
    send(wblk, wall.at[c, own_pos], b_s.at[0], b_r.at[0], plane(shifted(first, 1, 4), second))
    send(wblk, wall.at[c, own_pos], b_s.at[1], b_r.at[1], plane(shifted(first, -1, 4), second))

    arrived(got, p_sem.at[0], p_sem.at[1])
    a, b = mine[...], got[...]
    lo = jnp.where(even, a, b)
    hi = jnp.where(even, b, a)
    rows = jnp.concatenate([lo.astype(F32), hi.astype(F32)], axis=1).astype(BF)
    own_xc = (pl.ds(pl.multiple_of(lax.rem(z, 2) * 128, 128), 128),
              pl.ds(pl.multiple_of(lax.div(z, 2) * PAIR, 128), PAIR))
    xc[own_xc] = rows
    packed[:, 0:PAIR] = (dot(place_m[...], rows) * w_m[...]).astype(BF)
    pl_l = place_l[...]
    quarter = (iota((256, 128), 0) >> 2) & 3
    left = jnp.zeros((256, 256), F32)
    for q in range(4):
        sel = jnp.where(quarter == q, pl_l, jnp.zeros_like(pl_l))
        if q < 3:
            left = left + dot(sel, rows[:, 256 * q:256 * q + 256])
        else:
            last = dot(sel, rows[:, 768:896])
    wl = w_l[...]
    packed[:, PAIR:PAIR + 128] = ((left[:, 0:128] + last) * wl).astype(BF)
    packed[:, PAIR + 128:WIDE] = (left[:, 128:256] * wl).astype(BF)

    def rows16(ref, n):
        return ref.at[pl.ds(pl.multiple_of(16 * n, 16), 16), :]

    own_shard = shards.at[z, c]
    for k in range(1, 16):
        to = chip(k)
        send(rows16(packed, to), rows16(own_shard, j), c_s.at[k], c_r.at[k], (to * 2 + c, z))
    keep = pltpu.make_async_copy(rows16(packed, j), rows16(own_shard, j), loc.at[1])
    keep.start()
    here.wait()

    send(wall.at[c, own_pos], wall.at[c, own_pos], bm_s.at[0], bm_r.at[0], (sib, z))
    send(eg, sib_w.at[0], w_s.at[0], w_r.at[0], (sib, z))
    send(eu, sib_w.at[1], w_s.at[1], w_r.at[1], (sib, z))
    before = second * 4 + shifted(first, -1, 4)
    after = second * 4 + shifted(first, 1, 4)
    across = second * 4 + shifted(first, 2, 4)
    arrived(wall.at[c, before], b_s.at[0], b_r.at[0])
    send(block(before, 0), block(before, 0), b_s.at[2], b_r.at[2], plane(shifted(first, 1, 4), second))
    arrived(wall.at[c, after], b_s.at[1], b_r.at[1])
    send(block(after, 1), block(after, 1), b_s.at[3], b_r.at[3], plane(shifted(first, -1, 4), second))

    for k in range(1, 16):
        arrived(rows16(own_shard, chip_back(k)), c_s.at[k], c_r.at[k])
    keep.wait()

    right, left_z = shifted(z, 1, 8), shifted(z, -1, 8)

    def ring_start(view, half, s_sem, r_sem):
        send(view(z), view(z), s_sem.at[0], r_sem.at[0], (i, right))
        send(view(z), view(z), s_sem.at[4], r_sem.at[4], (i, left_z))

    def ring_step(view, half, s_sem, r_sem, s):
        o = shifted(z, -s, 8)
        arrived(view(o), s_sem.at[s - 1], r_sem.at[s - 1])
        part = view(o) if s < 3 else half(o, 0)
        send(part, part, s_sem.at[s], r_sem.at[s], (i, right))
        o = shifted(z, s, 8)
        arrived(view(o), s_sem.at[s + 3], r_sem.at[s + 3])
        part = view(o) if s < 3 else half(o, 1)
        send(part, part, s_sem.at[s + 4], r_sem.at[s + 4], (i, left_z))

    def ring_end(view, half, s_sem, r_sem):
        o = shifted(z, 4, 8)
        arrived(half(o, 0), s_sem.at[3], r_sem.at[3])
        arrived(half(o, 1), s_sem.at[7], r_sem.at[7])

    def shard(o):
        return shards.at[o, c]

    def shard_half(o, h):
        return shards.at[o, c, pl.ds(128 * h, 128), :]

    def mirror(s):
        o = shifted(z, s, 8)
        send(shards.at[o, c], shards.at[o, c], m_s.at[s], m_r.at[s], (sib, z))

    def group(g):
        return wall.at[c, pl.ds(g * 4, 4)]

    def group_half(g, h):
        return wall.at[c, pl.ds(g * 4 + 2 * h, 2)]

    ring_start(shard, shard_half, d_s, d_r)
    arrived(block(across, 0), b_s.at[2], b_r.at[2])
    arrived(block(across, 1), b_s.at[3], b_r.at[3])
    s_up, s_down, s_over = (shifted(second, 1, 4), shifted(second, -1, 4), shifted(second, 2, 4))
    send(group(second), group(second), b_s.at[4], b_r.at[4], plane(first, s_up))
    send(group(second), group(second), b_s.at[5], b_r.at[5], plane(first, s_down))
    mirror(0)
    send(wall.at[c, before], wall.at[c, before], bm_s.at[1], bm_r.at[1], (sib, z))
    send(wall.at[c, after], wall.at[c, after], bm_s.at[2], bm_r.at[2], (sib, z))
    send(wall.at[c, across], wall.at[c, across], bm_s.at[3], bm_r.at[3], (sib, z))

    ring_step(shard, shard_half, d_s, d_r, 1)
    mirror(1)
    mirror(7)
    ring_step(shard, shard_half, d_s, d_r, 2)
    mirror(2)
    mirror(6)
    arrived(group(s_down), b_s.at[4], b_r.at[4])
    send(group_half(s_down, 0), group_half(s_down, 0), b_s.at[6], b_r.at[6], plane(first, s_up))
    send(group(s_down), group(s_down), bm_s.at[4], bm_r.at[4], (sib, z))
    arrived(group(s_up), b_s.at[5], b_r.at[5])
    send(group_half(s_up, 1), group_half(s_up, 1), b_s.at[7], b_r.at[7], plane(first, s_down))
    send(group(s_up), group(s_up), bm_s.at[5], bm_r.at[5], (sib, z))
    ring_step(shard, shard_half, d_s, d_r, 3)

    def xc_view(o):
        return xc.at[pl.ds(pl.multiple_of(lax.rem(o, 2) * 128, 128), 128),
                     pl.ds(pl.multiple_of(lax.div(o, 2) * PAIR, 128), PAIR)]

    def xc_half(o, h):
        return xc.at[pl.ds(pl.multiple_of(lax.rem(o, 2) * 128 + 64 * h, 64), 64),
                     pl.ds(pl.multiple_of(lax.div(o, 2) * PAIR, 128), PAIR)]

    ring_start(xc_view, xc_half, a_s, a_r)
    mirror(3)
    mirror(5)
    ring_end(shard, shard_half, d_s, d_r)
    mirror(4)
    for s in range(8):
        o = shifted(z, s, 8)
        arrived(shards.at[o, 1 - c], m_s.at[s], m_r.at[s])

    r, k_ = iota((256, 256), 0), iota((256, 256), 1)
    unfold = onehot(k_ == ((r >> 2) & 15) * 16 + (r >> 6) * 4 + (r & 3))
    for zz in range(8):
        m, arr = zz // 2, zz % 2
        for cc in range(2):
            flat = dot(unfold, shards[zz, cc, :, PAIR:WIDE]).astype(BF)
            for q in range(4):
                n = 256 if q < 3 else 128
                lbuf[arr, 64 * cc:64 * cc + 64, PAIR * m + 256 * q:PAIR * m + 256 * q + n] = (
                    flat[64 * q:64 * q + 64, 0:n])

    def forward(load_t, load_c):
        gate = jnp.zeros((), F32)
        gate = up = grad = None
        for m in range(4):
            cols = slice(PAIR * m, PAIR * m + PAIR)
            t, ct = load_t(m), load_c(m)
            pg, pu, pd = dot(eg[:, cols], t, NT), dot(eu[:, cols], t, NT), dot(ed[:, cols], ct, NT)
            gate = pg if gate is None else gate + pg
            up = pu if up is None else up + pu
            grad = pd if grad is None else grad + pd
        silu, gg, gu = swiglu(gate, up, grad)
        return (silu * up).astype(BF), gg, gu

    for cc in range(2):
        h, gg, gu = forward(lambda m: shards[2 * m, cc, :, 0:PAIR], lambda m: shards[2 * m + 1, cc, :, 0:PAIR])
        hm[cc] = h
        grm[cc, 0] = gg
        grm[cc, 1] = gu
    h, gg, gu = forward(lambda m: lbuf[0, :, PAIR * m:PAIR * m + PAIR],
                        lambda m: lbuf[1, :, PAIR * m:PAIR * m + PAIR])
    hl[...] = h
    grl[0] = gg
    grl[1] = gu
    send(grm.at[1 - c], sib_m, g_s.at[0], g_r.at[0], (sib, z))
    send(grl, sib_l, g_s.at[1], g_r.at[1], (sib, z))
    ring_step(xc_view, xc_half, a_s, a_r, 1)

    r, k_ = iota((256, 256), 0), iota((256, 256), 1)
    eye = onehot(r == k_)
    pick = onehot(iota((64, 128), 1) == iota((64, 128), 0) + 64 * c)
    arrived(sib_w.at[0], w_s.at[0], w_r.at[0])
    arrived(sib_w.at[1], w_s.at[1], w_r.at[1])
    for n in range(2):
        tr[n, 0:256, :] = dot(eye, grm[c, n], NT).astype(BF)
        tr[n, 256:320, :] = dot(pick, grl[n], NT).astype(BF)
    arrived(sib_m, g_s.at[0], g_r.at[0])
    arrived(sib_l, g_s.at[1], g_r.at[1])
    for n in range(2):
        tr[2 + n, 0:256, :] = dot(eye, sib_m[n], NT).astype(BF)
        tr[2 + n, 256:320, :] = dot(pick, sib_l[n], NT).astype(BF)
    for m in range(4):
        cols = slice(PAIR * m, PAIR * m + PAIR)
        o = (dot(tr[0], eg[:, cols]) + dot(tr[1], eu[:, cols])
             + dot(tr[2], sib_w[0, :, cols]) + dot(tr[3], sib_w[1, :, cols])).astype(BF)
        fsend[:, cols] = o[0:256]
        lstack[64 * m:64 * m + 64, :] = o[256:320]
    fold = onehot(r == ((k_ >> 2) & 15) * 16 + (k_ >> 6) * 4 + (k_ & 3))
    fsend[:, 3584:BACK] = dot(fold, lstack[...]).astype(BF)
    for k in range(1, 16):
        to = chip(k)
        send(rows16(fsend, to), rows16(frecv, j), f_s.at[k], f_r.at[k], (to * 2 + c, z))
    keep = pltpu.make_async_copy(rows16(fsend, j), rows16(frecv, j), loc.at[2])
    keep.start()
    ring_step(xc_view, xc_half, a_s, a_r, 2)

    def wgrad(out, g0, g1, gl, arr):
        for m in range(4):
            cols = slice(PAIR * m, PAIR * m + PAIR)
            out[:, cols] = (dot(g0, shards[2 * m + arr, 0, :, 0:PAIR])
                            + dot(g1, shards[2 * m + arr, 1, :, 0:PAIR])
                            + dot(gl, lbuf[arr, :, cols])).astype(BF)

    wgrad(out_g, grm[0, 0], grm[1, 0], grl[0], 0)
    ring_step(xc_view, xc_half, a_s, a_r, 3)
    wgrad(out_u, grm[0, 1], grm[1, 1], grl[1], 0)
    wgrad(out_d, hm[0], hm[1], hl[...], 1)

    arrived(group_half(s_over, 0), b_s.at[6], b_r.at[6])
    arrived(group_half(s_over, 1), b_s.at[7], b_r.at[7])
    send(group(s_over), group(s_over), bm_s.at[6], bm_r.at[6], (sib, z))
    ring_end(xc_view, xc_half, a_s, a_r)
    sib_f = c * x + (1 - c) * y
    sib_s = c * y + (1 - c) * x
    o_c = 1 - c
    for n, f in enumerate((0, -1, 1, 2)):
        arrived(wall.at[o_c, sib_s * 4 + shifted(sib_f, f, 4)], bm_s.at[n], bm_r.at[n])
    for n, s in enumerate((-1, 1, 2)):
        arrived(wall.at[o_c, pl.ds(shifted(sib_s, s, 4) * 4, 4)], bm_s.at[4 + n], bm_r.at[4 + n])

    eye128 = onehot(iota((128, 128), 0) == iota((128, 128), 1))

    def dense_forward(n, carry):
        cc, g = lax.div(n, 4), lax.rem(n, 4)
        w = wall[cc, pl.ds(g * 4, 4)].reshape(256, 3584)
        p = dot(w, xc[...], NT)
        gate = p[:, 0:128]
        up = pltpu.roll(gate, 256 - ROWS, 0)
        grad = pltpu.roll(p[:, 128:256], 256 - 2 * ROWS, 0)
        _, gg, gu = swiglu(gate, up, grad)
        row = iota((256, 128), 0) & 63
        shift = pltpu.roll(gu.astype(F32), ROWS, 0)
        both = jnp.where(row < ROWS, gg.astype(F32), jnp.where(row < 2 * ROWS, shift, 0.0)).astype(BF)
        ggt[n] = dot(eye128, both, NT).astype(BF)
        return carry

    lax.fori_loop(0, 8, dense_forward, 0)

    for k in range(1, 16):
        arrived(rows16(frecv, chip_back(k)), f_s.at[k], f_r.at[k])
    keep.wait()
    cq = (iota((128, 256), 1) >> 2) & 3
    cl = comb_l[...]
    for m in range(4):
        cols = slice(PAIR * m, PAIR * m + PAIR)
        total = dot(comb_m[...], frecv[:, cols]) + dot(
            jnp.where(cq == m, cl, jnp.zeros_like(cl)), frecv[:, 3584:BACK])
        for n in range(8):
            cc, g = n // 4, n % 4
            w = wall[cc, 4 * g:4 * g + 4, :, cols].reshape(256, PAIR)
            total = total + dot(ggt[n], w)
        rs_send[2 * m] = total[:, 0:448].astype(BF)
        rs_send[2 * m + 1] = total[:, 448:PAIR].astype(BF)
    for s in range(1, 8):
        to = shifted(z, s, 8)
        send(rs_send.at[to], rs_recv.at[z], r_s.at[s], r_r.at[s], (i, to))
    acc = rs_send[z].astype(F32)
    for s in range(1, 8):
        o = shifted(z, -s, 8)
        arrived(rs_recv.at[o], r_s.at[s], r_r.at[s])
        acc = acc + rs_recv[o].astype(F32)
    out_x[...] = acc.astype(BF)
    for copy in pending:
        copy.wait_send()


def body(
    tokens, cotangent, routes, route_weights, dense_gate, dense_up, dense_down,
    expert_gate, expert_up, expert_down,
):
    z = lax.axis_index("tensor")
    even = z % 2 == 0
    mine = jnp.where(even, tokens, cotangent)
    other = jnp.where(even, cotangent, tokens)
    wblk = jnp.concatenate(
        [dense_gate[0], dense_up[0], dense_down[0], jnp.zeros((64 - 3 * ROWS, 3584), BF)], axis=0)

    ids = routes.reshape(-1)
    n = ids.shape[0]
    order = jnp.arange(n, dtype=jnp.int32)
    ranks = jnp.sum(
        ((ids[:, None] == ids[None, :]) & (order[None, :] < order[:, None])).astype(jnp.int32), axis=1
    ).reshape(routes.shape)
    slot = jnp.arange(256, dtype=jnp.int32)
    main = jnp.where(ranks < 16, routes * 16 + ranks, -1)
    rest = jnp.where(ranks >= 16, routes * 4 + ranks - 16, -1)
    rest_slot = (slot // 16) * 4 + slot % 4
    hit_m = [main[:, t] for t in range(2)]
    hit_l = [rest[:, t] for t in range(2)]
    weights = [jnp.where(even, 1.0, route_weights[:, t]) for t in range(2)]

    def place(hits, slots):
        masks = [h[None, :] == slots[:, None] for h in hits]
        w = sum(jnp.sum(jnp.where(mk, wt[None, :], 0.0), axis=1) for mk, wt in zip(masks, weights))
        return (masks[0] | masks[1]).astype(BF), w[:, None]

    def comb(hits, slots):
        return ((hits[0][:, None] == slots[None, :]) | (hits[1][:, None] == slots[None, :])).astype(BF)

    place_m, w_m = place(hit_m, slot)
    place_l, w_l = place(hit_l, rest_slot)
    comb_m, comb_l = comb(hit_m, slot), comb(hit_l, rest_slot)

    V = pltpu.VMEM
    sem = pltpu.SemaphoreType.DMA
    scratch = [
        V((128, 448), BF),
        V((256, WIDE), BF),
        V((8, 2, 256, WIDE), BF),
        V((2, 128, 3584), BF),
        V((2, 16, 64, 3584), BF),
        V((2, 152, 3584), BF),
        V((2, 2, 152, 256), BF),
        V((2, 152, 128), BF),
        V((2, 152, 256), BF),
        V((152, 128), BF),
        V((2, 152, 256), BF),
        V((2, 152, 128), BF),
        V((4, 320, 152), BF),
        V((256, PAIR), BF),
        V((256, BACK), BF),
        V((256, BACK), BF),
        V((256, 3584), BF),
        V((8, 128, 256), BF),
        V((8, 128, 448), BF),
        V((8, 128, 448), BF),
        sem((2,)), sem((16,)), sem((16,)), sem((8,)), sem((8,)), sem((8,)), sem((8,)),
        sem((8,)), sem((8,)), sem((7,)), sem((7,)), sem((2,)), sem((2,)),
        sem((2,)), sem((2,)), sem((16,)), sem((16,)), sem((8,)), sem((8,)), sem((8,)), sem((8,)),
        sem((3,)),
    ]
    vm = pl.BlockSpec(memory_space=pltpu.VMEM)
    return pl.pallas_call(
        kernel,
        out_shape=(
            jax.ShapeDtypeStruct((128, 448), BF),
            jax.ShapeDtypeStruct((152, 3584), BF),
            jax.ShapeDtypeStruct((152, 3584), BF),
            jax.ShapeDtypeStruct((152, 3584), BF),
        ),
        in_specs=[vm] * 12,
        out_specs=[vm] * 4,
        scratch_shapes=scratch,
        compiler_params=pltpu.CompilerParams(
            collective_id=0, has_side_effects=True, vmem_limit_bytes=62 * 2**20),
    )(mine, other, place_m, place_l, comb_m, comb_l, w_m, w_l, wblk, expert_gate, expert_up, expert_down)


def solution(mesh):
    rows = P(("expert", "tensor"), None)
    dense = P("tensor", "expert", None)
    return jax.shard_map(
        body,
        mesh=mesh,
        in_specs=(
            P("expert", "tensor"), P("expert", "tensor"), P("expert", None), P("expert", None),
            dense, dense, dense, rows, rows, rows,
        ),
        out_specs=(P("expert", "tensor"), rows, rows, rows),
        check_vma=False,
    )
```

```python
import jax
import jax.numpy as jnp
from jax import lax
from jax.experimental import pallas as pl
from jax.experimental.pallas import tpu as pltpu
from jax.sharding import PartitionSpec as P

MESH = pl.DeviceIdType.MESH
BF, F32 = jnp.bfloat16, jnp.float32
NT = (((1,), (1,)), ((), ()))
NN = (((1,), (0,)), ((), ()))
ROWS = 19
PAIR = 896
WIDE = 1152


def dot(a, b, dims=NN):
    return lax.dot_general(a, b, dims, preferred_element_type=F32)


def iota(shape, dim):
    return lax.broadcasted_iota(jnp.int32, shape, dim)


def onehot(mask):
    return jnp.where(mask, 1.0, 0.0).astype(BF)


def swiglu(gate, up, grad):
    sig = 1.0 / (1.0 + jnp.exp(-gate))
    silu = gate * sig
    slope = sig * (1.0 + gate * (1.0 - sig))
    return silu, (grad * up * slope).astype(BF), (grad * silu).astype(BF)


def route_masks(routes, weights, even, place_m, place_l, comb_m, comb_l, w_m, w_l):
    t0, t1 = iota((128, 128), 0), iota((128, 128), 1)
    eye = t0 == t1
    ids = routes[...].astype(F32)
    row = [ids[k:k + 1, :] for k in range(2)]
    col = [jnp.sum(jnp.where(eye, r, 0.0), axis=1, keepdims=True) for r in row]

    def count(same, ahead, axis):
        n = sum(jnp.where(s & ahead, 1.0, 0.0) for s in same)
        return jnp.sum(n, axis=axis, keepdims=True)

    row_rank = [count([c == r for c in col], t0 < t1, 0) for r in row]
    col_rank = [count([r == c for r in row], t1 < t0, 1) for c in col]

    def slots(ids, ranks):
        main = [jnp.where(k < 16, e * 16 + k, -1.0) for e, k in zip(ids, ranks)]
        rest = [jnp.where(k >= 16, e * 4 + k - 16, -1.0) for e, k in zip(ids, ranks)]
        return main, rest

    def fill(place, w, hits, slot):
        masks = [h == slot for h in hits]
        place[...] = onehot(masks[0] | masks[1])
        picked = sum(jnp.where(mk, weights[k:k + 1, :], 0.0) for k, mk in enumerate(masks))
        picked = jnp.sum(picked, axis=1, keepdims=True)
        w[...] = jnp.where(even, jnp.ones_like(picked), picked)

    main, rest = slots(row, row_rank)
    s = iota((256, 128), 0)
    fill(place_m, w_m, main, s.astype(F32))
    fill(place_l, w_l, rest, ((s >> 4) * 4 + (s & 3)).astype(F32))
    main, rest = slots(col, col_rank)
    s = iota((128, 256), 1)
    sf, sl = s.astype(F32), ((s >> 4) * 4 + (s & 3)).astype(F32)
    comb_m[...] = onehot((main[0] == sf) | (main[1] == sf))
    comb_l[...] = onehot((rest[0] == sl) | (rest[1] == sl))


def kernel(
    tok_in, cot_in, routes_in, weights_in, dg_in, du_in, dd_in, eg_in, eu_in, ed_in,
    out_x, out_g, out_u, out_d,
    tok, cot, routes, weights, dg, du, dd, eg, eu, ed, res, place_m, place_l, comb_m, comb_l, w_m, w_l, unfold, fold, wblk, oth, blk,
    packed, shards, lbuf, wall, sib_w, acc, accl, grm, grl, hm, hl, sib_m, sib_l,
    tr, fsend, frecv, xc, ggt, dense, rs_send, rs_recv,
    p_s, p_r, c_s, c_r, d_s, d_r, m_s, m_r, b_s, b_r, bm_s, bm_r, w_s, w_r,
    g_s, g_r, f_s, f_r, a_s, a_r, r_s, r_r, loc,
):
    i = lax.axis_index("expert")
    z = lax.axis_index("tensor")
    c = lax.rem(i, 2)
    j = lax.div(i, 2)
    y, x = lax.div(j, 4), lax.rem(j, 4)
    sib = i + 1 - 2 * c
    par = lax.rem(z, 2)
    even = par == 0
    first = (1 - c) * x + c * y
    second = (1 - c) * y + c * x

    def plane(f, s):
        yy = (1 - c) * s + c * f
        xx = (1 - c) * f + c * s
        return ((yy * 4 + xx) * 2 + c, z)

    def shifted(v, s, n):
        return lax.rem(v + s + n, n)

    pending = []

    def send(src, dst, s_sem, r_sem, n, dev):
        copy = pltpu.make_async_remote_copy(
            src_ref=src, dst_ref=dst, send_sem=s_sem.at[n], recv_sem=r_sem.at[n],
            device_id=dev, device_id_type=MESH,
        )
        copy.start()
        pending.append(copy)

    def arrived(ref, s_sem, r_sem, n):
        pltpu.make_async_remote_copy(
            src_ref=ref, dst_ref=ref, send_sem=s_sem.at[0], recv_sem=r_sem.at[n],
            device_id=(sib, z), device_id_type=MESH,
        ).wait_recv()

    def local(src, dst, n):
        copy = pltpu.make_async_copy(src, dst, loc.at[n])
        copy.start()
        return copy

    offsets = ((0, 0), (1, 0), (0, 1), (3, 0), (0, 3), (1, 1), (3, 3), (2, 0), (0, 2), (1, 3), (3, 1),
               (2, 1), (1, 2), (2, 3), (3, 2), (2, 2))

    def chip(k, sign=1):
        p, q = ((sign * v) % 4 for v in offsets[k])
        return (lax.rem(y + (1 - c) * q + c * p, 4) * 4 + lax.rem(x + (1 - c) * p + c * q, 4))

    def chip_back(k):
        return chip(k, -1)

    barrier = pltpu.get_barrier_semaphore()
    for k in range(1, 16):
        pl.semaphore_signal(barrier, inc=1, device_id=(chip(k) * 2 + c, z), device_id_type=MESH)
    pl.semaphore_signal(barrier, inc=1, device_id=(sib, z), device_id_type=MESH)
    for s in range(1, 8):
        pl.semaphore_signal(barrier, inc=1, device_id=(i, shifted(z, s, 8)), device_id_type=MESH)
    early = [local(src, dst, 12 + n) for n, (src, dst) in enumerate((
        (tok_in, tok), (cot_in, cot), (dg_in, dg), (du_in, du), (dd_in, dd),
        (routes_in, routes), (weights_in, weights)))]
    loads = [local(eg_in, eg, 0), local(eu_in, eu, 1), local(ed_in, ed, 2)]
    for copy in early:
        copy.wait()

    t, ct = tok[...], cot[...]
    half = pl.ds(pl.multiple_of(448 * par, 64), 448)
    oth[...] = jnp.where(even, ct, t)
    blk[half, :] = jnp.where(even, t, ct)
    at, k_ = iota((64, ROWS), 0), iota((64, ROWS), 1)
    wblk[...] = sum(
        dot(onehot(at == k_ + ROWS * n), m[0]) for n, m in enumerate((dg, du, dd))).astype(BF)
    pl.semaphore_wait(barrier, 23)

    partner = z + 1 - 2 * par
    send(oth, blk.at[half, :], p_s, p_r, 0, (i, partner))

    def block(pos, h):
        return wall.at[c, pos, pl.ds(32 * h, 32), :]

    own_pos = second * 4 + first
    here = local(wblk, wall.at[c, own_pos], 3)
    send(wblk, wall.at[c, own_pos], b_s, b_r, 0, plane(shifted(first, 1, 4), second))
    send(wblk, wall.at[c, own_pos], b_s, b_r, 1, plane(shifted(first, -1, 4), second))

    route_masks(routes, weights, even, place_m, place_l, comb_m, comb_l, w_m, w_l)
    r, k_ = iota((256, 256), 0), iota((256, 256), 1)
    unfold[...] = onehot(k_ == ((r >> 2) & 15) * 16 + (r >> 6) * 4 + (r & 3))
    fold[...] = onehot(r == ((k_ >> 2) & 15) * 16 + (k_ >> 6) * 4 + (k_ & 3))
    acc[...] = jnp.zeros_like(acc)
    accl[...] = jnp.zeros_like(accl)

    right, left_z = shifted(z, 1, 8), shifted(z, -1, 8)

    def ring_start(view, s_sem, r_sem):
        send(view(z), view(z), s_sem, r_sem, 0, (i, right))
        send(view(z), view(z), s_sem, r_sem, 4, (i, left_z))

    def ring_step(view, half, s_sem, r_sem, s):
        o = shifted(z, -s, 8)
        arrived(view(o), s_sem, r_sem, s - 1)
        part = view(o) if s < 3 else half(o, 0)
        send(part, part, s_sem, r_sem, s, (i, right))
        o = shifted(z, s, 8)
        arrived(view(o), s_sem, r_sem, s + 3)
        part = view(o) if s < 3 else half(o, 1)
        send(part, part, s_sem, r_sem, s + 4, (i, left_z))

    def ring_end(half, s_sem, r_sem):
        o = shifted(z, 4, 8)
        arrived(half(o, 0), s_sem, r_sem, 3)
        arrived(half(o, 1), s_sem, r_sem, 7)

    def xc_cols(o):
        return pl.ds(pl.multiple_of(lax.div(o, 2) * PAIR, 128), PAIR)

    def xc_view(o):
        return xc.at[pl.ds(pl.multiple_of(lax.rem(o, 2) * 128, 128), 128), xc_cols(o)]

    def xc_half(o, h):
        return xc.at[pl.ds(pl.multiple_of(lax.rem(o, 2) * 128 + 64 * h, 64), 64), xc_cols(o)]

    eye128 = onehot(iota((128, 128), 0) == iota((128, 128), 1))
    arrived(blk.at[pl.ds(pl.multiple_of(448 * (1 - par), 64), 448), :], p_s, p_r, 0)
    xc[pl.ds(pl.multiple_of(par * 128, 128), 128), xc_cols(z)] = dot(eye128, blk[...], NT).astype(BF)
    ring_start(xc_view, a_s, a_r)

    packed[:, 0:PAIR] = (dot(place_m[...], blk[...], NT) * w_m[...]).astype(BF)
    quarter = (iota((256, 128), 0) >> 2) & 3
    sel = [jnp.where(quarter == q, place_l[...], jnp.zeros((256, 128), BF)) for q in range(4)]
    left = [sum(dot(sel[q], blk[256 * q + 128 * h:256 * q + 128 * h + 128, :], NT)
                for q in range(4) if 256 * q + 128 * h < PAIR) for h in range(2)]
    for h in range(2):
        packed[:, PAIR + 128 * h:PAIR + 128 * h + 128] = (left[h] * w_l[...]).astype(BF)

    def rows16(ref, n):
        return ref.at[pl.ds(pl.multiple_of(16 * n, 16), 16), :]

    own_shard = shards.at[z, c]
    for k in range(1, 16):
        to = chip(k)
        send(rows16(packed, to), rows16(own_shard, j), c_s, c_r, k, (to * 2 + c, z))
    keep = local(rows16(packed, j), rows16(own_shard, j), 4)
    here.wait()
    send(wall.at[c, own_pos], wall.at[c, own_pos], bm_s, bm_r, 0, (sib, z))
    for copy in loads:
        copy.wait()
    send(eg, sib_w.at[0], w_s, w_r, 0, (sib, z))
    send(eu, sib_w.at[1], w_s, w_r, 1, (sib, z))

    before = second * 4 + shifted(first, -1, 4)
    after = second * 4 + shifted(first, 1, 4)
    across = second * 4 + shifted(first, 2, 4)
    arrived(wall.at[c, before], b_s, b_r, 0)
    send(block(before, 0), block(before, 0), b_s, b_r, 2, plane(shifted(first, 1, 4), second))
    arrived(wall.at[c, after], b_s, b_r, 1)
    send(block(after, 1), block(after, 1), b_s, b_r, 3, plane(shifted(first, -1, 4), second))
    ring_step(xc_view, xc_half, a_s, a_r, 1)
    for k in range(1, 16):
        arrived(rows16(own_shard, chip_back(k)), c_s, c_r, k)
    keep.wait()

    def shard_half(o, h):
        return shards.at[o, c, pl.ds(128 * h, 128), :]

    def mirror(s):
        o = shifted(z, s, 8)
        send(shards.at[o, c], shards.at[o, c], m_s, m_r, s, (sib, z))

    def group(g):
        return wall.at[c, pl.ds(g * 4, 4)]

    def group_half(g, h):
        return wall.at[c, pl.ds(g * 4 + 2 * h, 2)]

    def right_hop(s, h):
        o = shifted(z, -s, 8)
        if s:
            arrived(shard_half(o, h), d_s, d_r, 2 * s - 2 + h)
        if s < 3 or h == 0:
            send(shard_half(o, h), shard_half(o, h), d_s, d_r, 2 * s + h, (i, right))

    def left_hop(s, h):
        o = shifted(z, s, 8)
        if s:
            arrived(shard_half(o, h), d_s, d_r, 8 + 2 * s - 2 + h)
        if s < 3 or h == 1:
            send(shard_half(o, h), shard_half(o, h), d_s, d_r, 8 + 2 * s + h, (i, left_z))

    def hop(s, part):
        right_hop(s, part)
        left_hop(s, 1 - part)

    hop(0, 0)
    hop(0, 1)
    arrived(block(across, 0), b_s, b_r, 2)
    arrived(block(across, 1), b_s, b_r, 3)
    s_up, s_down, s_over = (shifted(second, 1, 4), shifted(second, -1, 4), shifted(second, 2, 4))
    send(group(second), group(second), b_s, b_r, 4, plane(first, s_up))
    send(group(second), group(second), b_s, b_r, 5, plane(first, s_down))
    mirror(0)
    send(wall.at[c, before], wall.at[c, before], bm_s, bm_r, 1, (sib, z))
    send(wall.at[c, after], wall.at[c, after], bm_s, bm_r, 2, (sib, z))
    send(wall.at[c, across], wall.at[c, across], bm_s, bm_r, 3, (sib, z))

    def absorb(s):
        o = shifted(z, s, 8)
        arrived(shards.at[o, 1 - c], m_s, m_r, s)
        base = lax.div(o, 2) * PAIR
        cols = pl.ds(pl.multiple_of(base, 128), PAIR)
        arr = lax.rem(o, 2)
        for cc in range(2):
            flat = dot(unfold[...], shards[o, cc, :, PAIR:WIDE]).astype(BF)
            for q in range(4):
                n = 256 if q < 3 else 128
                lbuf[arr, 64 * cc:64 * cc + 64, pl.ds(pl.multiple_of(base + 256 * q, 128), n)] = (
                    flat[64 * q:64 * q + 64, 0:n])

        def add(n, w):
            wc = w[:, cols]
            for cc in range(2):
                acc[n, cc] += dot(wc, shards[o, cc, :, 0:PAIR], NT)
            accl[n] += dot(wc, lbuf[arr, :, cols], NT)

        @pl.when(arr == 0)
        def _():
            add(0, eg)
            add(1, eu)

        @pl.when(arr == 1)
        def _():
            add(2, ed)

    o_c = 1 - c
    sib_f = c * x + (1 - c) * y
    sib_s = c * y + (1 - c) * x

    def dense_forward(cc, g):
        w = wall[cc, pl.ds(g * 4, 4)].reshape(256, 3584)
        p = dot(w, xc[...], NT)
        gate = p[:, 0:128]
        up = pltpu.roll(gate, 256 - ROWS, 0)
        grad = pltpu.roll(p[:, 128:256], 256 - 2 * ROWS, 0)
        _, gg, gu = swiglu(gate, up, grad)
        row = iota((256, 128), 0) & 63
        shift = pltpu.roll(gu.astype(F32), ROWS, 0)
        both = jnp.where(row < ROWS, gg.astype(F32), jnp.where(row < 2 * ROWS, shift, 0.0)).astype(BF)
        ggt[cc * 4 + g] = dot(eye128, both, NT).astype(BF)

    def dense_back(n, carry):
        cols = pl.ds(pl.multiple_of(n * 512, 128), 512)
        dense[:, cols] = sum(
            dot(ggt[k], wall[k // 4, 4 * (k % 4):4 * (k % 4) + 4, :, cols].reshape(256, 512))
            for k in range(8))
        return carry

    ring_step(xc_view, xc_half, a_s, a_r, 2)
    absorb(0)
    hop(1, 0)
    ring_step(xc_view, xc_half, a_s, a_r, 3)
    hop(1, 1)
    mirror(1)
    mirror(7)
    absorb(1)
    absorb(7)
    hop(2, 0)
    arrived(group(s_down), b_s, b_r, 4)
    send(group_half(s_down, 0), group_half(s_down, 0), b_s, b_r, 6, plane(first, s_up))
    send(group(s_down), group(s_down), bm_s, bm_r, 4, (sib, z))
    arrived(group(s_up), b_s, b_r, 5)
    send(group_half(s_up, 1), group_half(s_up, 1), b_s, b_r, 7, plane(first, s_down))
    send(group(s_up), group(s_up), bm_s, bm_r, 5, (sib, z))
    hop(2, 1)
    mirror(2)
    mirror(6)
    ring_end(xc_half, a_s, a_r)
    for n, f in enumerate((0, -1, 1, 2)):
        arrived(wall.at[o_c, sib_s * 4 + shifted(sib_f, f, 4)], bm_s, bm_r, n)
    dense_forward(c, second)
    dense_forward(o_c, sib_s)
    absorb(2)
    absorb(6)
    hop(3, 0)
    arrived(group_half(s_over, 0), b_s, b_r, 6)
    arrived(group_half(s_over, 1), b_s, b_r, 7)
    send(group(s_over), group(s_over), bm_s, bm_r, 6, (sib, z))
    dense_forward(c, s_down)
    dense_forward(c, s_up)
    for n, s in enumerate((-1, 1)):
        g = shifted(sib_s, s, 4)
        arrived(wall.at[o_c, pl.ds(g * 4, 4)], bm_s, bm_r, 4 + n)
        dense_forward(o_c, g)
    hop(3, 1)
    mirror(3)
    mirror(5)
    absorb(3)
    absorb(5)
    arrived(shard_half(shifted(z, 4, 8), 0), d_s, d_r, 6)
    arrived(shard_half(shifted(z, 4, 8), 1), d_s, d_r, 15)
    mirror(4)
    absorb(4)

    for cc in range(2):
        silu, gg, gu = swiglu(acc[0, cc], acc[1, cc], acc[2, cc])
        hm[cc] = (silu * acc[1, cc]).astype(BF)
        grm[cc, 0] = gg
        grm[cc, 1] = gu
    silu, gg, gu = swiglu(accl[0], accl[1], accl[2])
    hl[...] = (silu * accl[1]).astype(BF)
    grl[0] = gg
    grl[1] = gu
    send(grm.at[1 - c], sib_m, g_s, g_r, 0, (sib, z))
    send(grl, sib_l, g_s, g_r, 1, (sib, z))

    eye = onehot(iota((256, 256), 0) == iota((256, 256), 1))
    pick = onehot(iota((64, 128), 1) == iota((64, 128), 0) + 64 * c)
    arrived(sib_w.at[0], w_s, w_r, 0)
    arrived(sib_w.at[1], w_s, w_r, 1)
    for n in range(2):
        tr[n, 0:256, :] = dot(eye, grm[c, n], NT).astype(BF)
        tr[n, 256:320, :] = dot(pick, grl[n], NT).astype(BF)
    arrived(sib_m, g_s, g_r, 0)
    arrived(sib_l, g_s, g_r, 1)
    for n in range(2):
        tr[2 + n, 0:256, :] = dot(eye, sib_m[n], NT).astype(BF)
        tr[2 + n, 256:320, :] = dot(pick, sib_l[n], NT).astype(BF)

    pair = lax.div(z, 2)
    chunk = [shifted(pair, 1 + k, 4) for k in range(4)]
    keeps = []
    for k in range(4):
        cols = pl.ds(pl.multiple_of(chunk[k] * PAIR, 128), PAIR)
        o = (dot(tr[0], eg[:, cols]) + dot(tr[1], eu[:, cols])
             + dot(tr[2], sib_w[0, :, cols]) + dot(tr[3], sib_w[1, :, cols])).astype(BF)
        fsend[k, :, 0:PAIR] = o[0:256]
        tail = o[256:320]
        stack = jnp.concatenate(
            [tail[:, 0:256], tail[:, 256:512], tail[:, 512:768],
             jnp.concatenate([tail[:, 768:896], jnp.zeros((64, 128), BF)], axis=1)], axis=0)
        fsend[k, :, PAIR:WIDE] = dot(fold[...], stack).astype(BF)
        for n in range(1, 16):
            to = chip(n)
            send(rows16(fsend.at[k], to), rows16(frecv.at[k], j), f_s, f_r, 16 * k + n, (to * 2 + c, z))
        keeps.append(local(rows16(fsend.at[k], j), rows16(frecv.at[k], j), 5 + k))

    outs = []

    def wgrad(n, out, g0, g1, gl, arr):
        def cols_of(m, carry):
            cols = pl.ds(pl.multiple_of(m * PAIR, 128), PAIR)
            res[n, :, cols] = (dot(g0, shards[2 * m + arr, 0, :, 0:PAIR])
                               + dot(g1, shards[2 * m + arr, 1, :, 0:PAIR])
                               + dot(gl, lbuf[arr, :, cols])).astype(BF)
            return carry

        lax.fori_loop(0, 4, cols_of, 0)
        outs.append(local(res.at[n], out, 9 + n))

    cq = (iota((128, 256), 1) >> 2) & 3

    def combine(k):
        for n in range(1, 16):
            arrived(rows16(frecv.at[k], chip_back(n)), f_s, f_r, 16 * k + n)
        keeps[k].wait()
        m = chunk[k]
        total = dense[:, pl.ds(pl.multiple_of(m * PAIR, 128), PAIR)] + dot(comb_m[...], frecv[k, :, 0:PAIR])
        parts = []
        for q in range(4):
            n = 256 if q < 3 else 128
            sel = jnp.where(cq == q, comb_l[...], jnp.zeros((128, 256), BF))
            parts.append(dot(sel, frecv[k, :, PAIR:PAIR + n]))
        total = total + jnp.concatenate(parts, axis=1)
        flip = total.T.astype(BF)
        for h in range(2):
            rs_send[2 * m + h] = flip[448 * h:448 * h + 448]
        if k < 3:
            for h in range(2):
                to = 2 * m + h
                copy = pltpu.make_async_remote_copy(
                    src_ref=rs_send.at[to], dst_ref=rs_recv.at[z], send_sem=r_s.at[2 * k + h],
                    recv_sem=r_r.at[2 * k + par], device_id=(i, to), device_id_type=MESH)
                copy.start()
                pending.append(copy)
        else:
            send(rs_send.at[partner], rs_recv.at[z], r_s, r_r, 6, (i, partner))

    dense_forward(c, s_over)
    g = shifted(sib_s, 2, 4)
    arrived(wall.at[o_c, pl.ds(g * 4, 4)], bm_s, bm_r, 6)
    dense_forward(o_c, g)
    lax.fori_loop(0, 7, dense_back, 0)
    wgrad(0, out_g, grm[0, 0], grm[1, 0], grl[0], 0)
    combine(0)
    wgrad(1, out_u, grm[0, 1], grm[1, 1], grl[1], 0)
    combine(1)
    wgrad(2, out_d, hm[0], hm[1], hl[...], 1)
    combine(2)
    combine(3)
    total = rs_send[z].astype(F32)
    for k in range(3):
        for h in range(2):
            o = 2 * shifted(pair, -1 - k, 4) + h
            arrived(rs_recv.at[o], r_s, r_r, 2 * k + h)
            total = total + rs_recv[o].astype(F32)
    arrived(rs_recv.at[partner], r_s, r_r, 6)
    out_x[...] = (total + rs_recv[partner].astype(F32)).astype(BF)
    for copy in pending:
        copy.wait_send()
    for copy in outs:
        copy.wait()


def copy_out(a, b, c, d, oa, ob, oc, od, va, vb, vc, vd, sems):
    arrays = ((a, va, oa), (b, vb, ob), (c, vc, oc), (d, vd, od))
    loads = [pltpu.make_async_copy(s, v, sems.at[n]) for n, (s, v, _) in enumerate(arrays)]
    stores = [pltpu.make_async_copy(v, t, sems.at[4 + n]) for n, (_, v, t) in enumerate(arrays)]
    for copy in loads:
        copy.start()
    for load, store in zip(loads, stores):
        load.wait()
        store.start()
    for store in stores:
        store.wait()


def body(
    tokens, cotangent, routes, route_weights, dense_gate, dense_up, dense_down,
    expert_gate, expert_up, expert_down,
):
    V = pltpu.VMEM
    scratch = [
        V((448, 128), BF), V((448, 128), BF),
        V((2, 128), jnp.int32), V((2, 128), F32),
        V((1, ROWS, 3584), BF), V((1, ROWS, 3584), BF), V((1, ROWS, 3584), BF),
        V((152, 3584), BF), V((152, 3584), BF), V((152, 3584), BF),
        V((3, 152, 3584), BF),
        V((256, 128), BF), V((256, 128), BF),
        V((128, 256), BF), V((128, 256), BF),
        V((256, 1), F32), V((256, 1), F32),
        V((256, 256), BF), V((256, 256), BF),
        V((64, 3584), BF),
        V((448, 128), BF),
        V((896, 128), BF),
        V((256, WIDE), BF),
        V((8, 2, 256, WIDE), BF),
        V((2, 128, 3584), BF),
        V((2, 16, 64, 3584), BF),
        V((2, 152, 3584), BF),
        V((3, 2, 152, 256), F32),
        V((3, 152, 128), F32),
        V((2, 2, 152, 256), BF),
        V((2, 152, 128), BF),
        V((2, 152, 256), BF),
        V((152, 128), BF),
        V((2, 152, 256), BF),
        V((2, 152, 128), BF),
        V((4, 320, 152), BF),
        V((4, 256, WIDE), BF),
        V((4, 256, WIDE), BF),
        V((256, 3584), BF),
        V((8, 128, 256), BF),
        V((128, 3584), F32),
        V((8, 448, 128), BF),
        V((8, 448, 128), BF),
    ]
    for n in (1, 16, 16, 8, 8, 7, 2, 2, 64, 8, 7):
        scratch += [pltpu.SemaphoreType.DMA((n,))] * 2
    scratch.append(pltpu.SemaphoreType.DMA((19,)))
    vm = pl.BlockSpec(memory_space=pltpu.VMEM)
    hbm = pl.BlockSpec(memory_space=pl.ANY)
    shapes = (jax.ShapeDtypeStruct((448, 128), BF),) + (jax.ShapeDtypeStruct((152, 3584), BF),) * 3
    results = pl.pallas_call(
        kernel,
        out_shape=shapes,
        in_specs=[hbm] * 10,
        out_specs=[vm] + [hbm] * 3,
        scratch_shapes=scratch,
        compiler_params=pltpu.CompilerParams(
            collective_id=0, has_side_effects=True, vmem_limit_bytes=62 * 2**20),
    )(tokens.T, cotangent.T, routes.T, route_weights.T, dense_gate, dense_up, dense_down,
      expert_gate, expert_up, expert_down)
    x, g, u, d = pl.pallas_call(
        copy_out,
        out_shape=shapes,
        in_specs=[hbm] * 4,
        out_specs=[hbm] * 4,
        scratch_shapes=[V(s.shape, BF) for s in shapes] + [pltpu.SemaphoreType.DMA((8,))],
        compiler_params=pltpu.CompilerParams(vmem_limit_bytes=62 * 2**20),
    )(*results)
    return x.T, g, u, d


def solution(mesh):
    rows = P(("expert", "tensor"), None)
    dense = P("tensor", "expert", None)
    return jax.shard_map(
        body,
        mesh=mesh,
        in_specs=(
            P("expert", "tensor"), P("expert", "tensor"), P("expert", None), P("expert", None),
            dense, dense, dense, rows, rows, rows,
        ),
        out_specs=(P("expert", "tensor"), rows, rows, rows),
        check_vma=False,
    )
```

```python
import jax
import jax.numpy as jnp
from jax import lax
from jax.experimental import pallas as pl
from jax.experimental.pallas import tpu as pltpu
from jax.sharding import PartitionSpec as P

MESH = pl.DeviceIdType.MESH
BF, F32 = jnp.bfloat16, jnp.float32
NT = (((1,), (1,)), ((), ()))
NN = (((1,), (0,)), ((), ()))
ROWS = 19
PAIR = 896
WIDE = 1152


def dot(a, b, dims=NN):
    return lax.dot_general(a, b, dims, preferred_element_type=F32)


def iota(shape, dim):
    return lax.broadcasted_iota(jnp.int32, shape, dim)


def onehot(mask):
    return jnp.where(mask, 1.0, 0.0).astype(BF)


def swiglu(gate, up, grad):
    sig = 1.0 / (1.0 + jnp.exp(-gate))
    silu = gate * sig
    slope = sig * (1.0 + gate * (1.0 - sig))
    return silu, (grad * up * slope).astype(BF), (grad * silu).astype(BF)


def route_masks(routes, weights, even, place_m, place_l, comb_m, comb_l, w_m, w_l):
    t0, t1 = iota((128, 128), 0), iota((128, 128), 1)
    eye = t0 == t1
    ids = routes[...].astype(F32)
    row = [ids[k:k + 1, :] for k in range(2)]
    col = [jnp.sum(jnp.where(eye, r, 0.0), axis=1, keepdims=True) for r in row]

    def count(same, ahead, axis):
        n = sum(jnp.where(s & ahead, 1.0, 0.0) for s in same)
        return jnp.sum(n, axis=axis, keepdims=True)

    row_rank = [count([c == r for c in col], t0 < t1, 0) for r in row]
    col_rank = [count([r == c for r in row], t1 < t0, 1) for c in col]

    def slots(ids, ranks):
        main = [jnp.where(k < 16, e * 16 + k, -1.0) for e, k in zip(ids, ranks)]
        rest = [jnp.where(k >= 16, e * 4 + k - 16, -1.0) for e, k in zip(ids, ranks)]
        return main, rest

    def fill(place, w, hits, slot):
        masks = [h == slot for h in hits]
        place[...] = onehot(masks[0] | masks[1])
        picked = sum(jnp.where(mk, weights[k:k + 1, :], 0.0) for k, mk in enumerate(masks))
        picked = jnp.sum(picked, axis=1, keepdims=True)
        w[...] = jnp.where(even, jnp.ones_like(picked), picked)

    main, rest = slots(row, row_rank)
    s = iota((256, 128), 0)
    fill(place_m, w_m, main, s.astype(F32))
    fill(place_l, w_l, rest, ((s >> 4) * 4 + (s & 3)).astype(F32))
    main, rest = slots(col, col_rank)
    s = iota((128, 256), 1)
    sf, sl = s.astype(F32), ((s >> 4) * 4 + (s & 3)).astype(F32)
    comb_m[...] = onehot((main[0] == sf) | (main[1] == sf))
    comb_l[...] = onehot((rest[0] == sl) | (rest[1] == sl))


def kernel(
    tok_in, cot_in, routes_in, weights_in, dg_in, du_in, dd_in, eg_in, eu_in, ed_in,
    out_x, out_g, out_u, out_d,
    tok, cot, routes, weights, dg, du, dd, eg, eu, ed, res, place_m, place_l, comb_m, comb_l, w_m, w_l, unfold, fold, wblk, blk,
    packed, shards, lbuf, wall, sib_w, acc, accl, grm, grl, hm, hl, sib_m, sib_l,
    tr, fsend, frecv, xt, ggt, dense, own_sum, rs_send, rs_recv,
    c_s, c_r, d_s, d_r, m_s, m_r, b_s, b_r, bm_s, bm_r, w_s, w_r,
    g_s, g_r, f_s, f_r, a_s, a_r, r_s, r_r, loc,
):
    i = lax.axis_index("expert")
    z = lax.axis_index("tensor")
    c = lax.rem(i, 2)
    j = lax.div(i, 2)
    y, x = lax.div(j, 4), lax.rem(j, 4)
    sib = i + 1 - 2 * c
    par = lax.rem(z, 2)
    even = par == 0
    first = (1 - c) * x + c * y
    second = (1 - c) * y + c * x

    def plane(f, s):
        yy = (1 - c) * s + c * f
        xx = (1 - c) * f + c * s
        return ((yy * 4 + xx) * 2 + c, z)

    def shifted(v, s, n):
        return lax.rem(v + s + n, n)

    pending = []

    def send(src, dst, s_sem, r_sem, n, dev):
        copy = pltpu.make_async_remote_copy(
            src_ref=src, dst_ref=dst, send_sem=s_sem.at[n], recv_sem=r_sem.at[n],
            device_id=dev, device_id_type=MESH,
        )
        copy.start()
        pending.append(copy)

    def arrived(ref, s_sem, r_sem, n):
        pltpu.make_async_remote_copy(
            src_ref=ref, dst_ref=ref, send_sem=s_sem.at[0], recv_sem=r_sem.at[n],
            device_id=(sib, z), device_id_type=MESH,
        ).wait_recv()

    def local(src, dst, n):
        copy = pltpu.make_async_copy(src, dst, loc.at[n])
        copy.start()
        return copy

    offsets = ((0, 0), (1, 1), (3, 3), (1, 3), (3, 1), (2, 0), (0, 2), (2, 2),
               (1, 0), (0, 1), (3, 0), (0, 3), (2, 1), (1, 2), (2, 3), (3, 2))

    def chip(k, sign=1):
        p, q = ((sign * v) % 4 for v in offsets[k])
        return (lax.rem(y + (1 - c) * q + c * p, 4) * 4 + lax.rem(x + (1 - c) * p + c * q, 4))

    barrier = pltpu.get_barrier_semaphore()
    for k in range(1, 16):
        pl.semaphore_signal(barrier, inc=1, device_id=(chip(k) * 2 + c, z), device_id_type=MESH)
    pl.semaphore_signal(barrier, inc=1, device_id=(sib, z), device_id_type=MESH)
    for s in range(1, 8):
        pl.semaphore_signal(barrier, inc=1, device_id=(i, shifted(z, s, 8)), device_id_type=MESH)
    early = [local(src, dst, 12 + n) for n, (src, dst) in enumerate((
        (tok_in, tok), (cot_in, cot), (dg_in, dg), (du_in, du), (dd_in, dd),
        (routes_in, routes), (weights_in, weights)))]
    loads = [local(eg_in, eg, 0), local(eu_in, eu, 1), local(ed_in, ed, 2)]
    for copy in early:
        copy.wait()

    xt[z, :, 0:128] = tok[...]
    xt[z, :, 128:256] = cot[...]
    at, k_ = iota((64, ROWS), 0), iota((64, ROWS), 1)
    wblk[...] = sum(
        dot(onehot(at == k_ + ROWS * n), m[0]) for n, m in enumerate((dg, du, dd))).astype(BF)
    pl.semaphore_wait(barrier, 23)

    right, left_z = shifted(z, 1, 8), shifted(z, -1, 8)

    def lanes(o, n):
        return xt.at[o, :, pl.ds(pl.multiple_of(128 * n, 128), 128)]

    def xt_half(o, h):
        return xt.at[o, pl.ds(224 * h, 224), :]

    for n, lane in enumerate((1 - par, par)):
        send(lanes(z, lane), lanes(z, lane), a_s, a_r, n, (i, right))
        send(lanes(z, lane), lanes(z, lane), a_s, a_r, 5 + n, (i, left_z))

    def ring_step(s):
        for base, sign, dev in ((0, -1, (i, right)), (5, 1, (i, left_z))):
            o = shifted(z, sign * s, 8)
            if s == 1:
                arrived(lanes(o, 1 - par), a_s, a_r, base + 1)
            else:
                arrived(xt.at[o], a_s, a_r, base + s)
            part = xt.at[o] if s < 3 else xt_half(o, 0 if base == 0 else 1)
            send(part, part, a_s, a_r, base + s + 1, dev)

    def ring_end():
        o = shifted(z, 4, 8)
        arrived(xt_half(o, 0), a_s, a_r, 4)
        arrived(xt_half(o, 1), a_s, a_r, 9)

    def block(pos, h):
        return wall.at[c, pos, pl.ds(32 * h, 32), :]

    own_pos = second * 4 + first
    here = local(wblk, wall.at[c, own_pos], 3)
    send(wblk, wall.at[c, own_pos], b_s, b_r, 0, plane(shifted(first, 1, 4), second))
    send(wblk, wall.at[c, own_pos], b_s, b_r, 1, plane(shifted(first, -1, 4), second))

    route_masks(routes, weights, even, place_m, place_l, comb_m, comb_l, w_m, w_l)
    r, k_ = iota((256, 256), 0), iota((256, 256), 1)
    unfold[...] = onehot(k_ == ((r >> 2) & 15) * 16 + (r >> 6) * 4 + (r & 3))
    r, k_ = iota((128, 128), 0), iota((128, 128), 1)
    fold[...] = onehot(r == ((k_ >> 2) & 7) * 16 + (k_ >> 5) * 4 + (k_ & 3))
    acc[...] = jnp.zeros_like(acc)
    accl[...] = jnp.zeros_like(accl)

    eye128 = onehot(iota((128, 128), 0) == iota((128, 128), 1))
    pair = lax.div(z, 2)
    arrived(lanes(shifted(z, -1, 8), par), a_s, a_r, 0)
    arrived(lanes(shifted(z, 1, 8), par), a_s, a_r, 5)
    for h in range(2):
        blk[448 * h:448 * h + 448, :] = xt[2 * pair + h, :, pl.ds(pl.multiple_of(128 * par, 128), 128)]

    packed[:, 0:PAIR] = (dot(place_m[...], blk[...], NT) * w_m[...]).astype(BF)
    quarter = (iota((256, 128), 0) >> 2) & 3
    sel = [jnp.where(quarter == q, place_l[...], jnp.zeros((256, 128), BF)) for q in range(4)]
    left = [sum(dot(sel[q], blk[256 * q + 128 * h:256 * q + 128 * h + 128, :], NT)
                for q in range(4) if 256 * q + 128 * h < PAIR) for h in range(2)]
    for h in range(2):
        packed[:, PAIR + 128 * h:PAIR + 128 * h + 128] = (left[h] * w_l[...]).astype(BF)

    def rows16(ref, n):
        return ref.at[pl.ds(pl.multiple_of(16 * n, 16), 16), :]

    def own_rows(k):
        return shards.at[z, k // 8, c, pl.ds(16 * (k % 8), 16), :]

    for k in range(1, 16):
        to = chip(k)
        send(rows16(packed, to), own_rows(k), c_s, c_r, k, (to * 2 + c, z))
    keep = local(rows16(packed, j), own_rows(0), 4)
    here.wait()
    send(wall.at[c, own_pos], wall.at[c, own_pos], bm_s, bm_r, 0, (sib, z))
    for copy in loads:
        copy.wait()
    send(eg, sib_w.at[0], w_s, w_r, 0, (sib, z))
    send(eu, sib_w.at[1], w_s, w_r, 1, (sib, z))

    before = second * 4 + shifted(first, -1, 4)
    after = second * 4 + shifted(first, 1, 4)
    across = second * 4 + shifted(first, 2, 4)
    arrived(wall.at[c, before], b_s, b_r, 0)
    send(block(before, 0), block(before, 0), b_s, b_r, 2, plane(shifted(first, 1, 4), second))
    arrived(wall.at[c, after], b_s, b_r, 1)
    send(block(after, 1), block(after, 1), b_s, b_r, 3, plane(shifted(first, -1, 4), second))
    ring_step(1)

    def shard(o, h):
        return shards.at[o, h, c]

    def shard_part(o, h, p):
        return shards.at[o, h, c, pl.ds(64 * p, 64), :]

    def mirror(s, h):
        o = shifted(z, s, 8)
        send(shard(o, h), shard(o, h), m_s, m_r, 2 * s + h, (sib, z))

    def hop(s, h):
        for base, sign, dev in ((8 * h, -1, (i, right)), (8 * h + 4, 1, (i, left_z))):
            o = shifted(z, sign * s, 8)
            if s:
                arrived(shard(o, h), d_s, d_r, base + s - 1)
            part = shard(o, h) if s < 3 else shard_part(o, h, 0 if sign < 0 else 1)
            send(part, part, d_s, d_r, base + s, dev)
        if s:
            mirror(s, h)
            mirror(8 - s, h)

    def hop_end(h):
        o = shifted(z, 4, 8)
        arrived(shard_part(o, h, 0), d_s, d_r, 8 * h + 3)
        arrived(shard_part(o, h, 1), d_s, d_r, 8 * h + 7)
        mirror(4, h)

    keep.wait()
    for k in range(1, 8):
        arrived(own_rows(k), c_s, c_r, k)
    hop(0, 0)
    for k in range(8, 16):
        arrived(own_rows(k), c_s, c_r, k)

    def group(g):
        return wall.at[c, pl.ds(g * 4, 4)]

    def group_half(g, h):
        return wall.at[c, pl.ds(g * 4 + 2 * h, 2)]

    arrived(block(across, 0), b_s, b_r, 2)
    arrived(block(across, 1), b_s, b_r, 3)
    s_up, s_down, s_over = (shifted(second, 1, 4), shifted(second, -1, 4), shifted(second, 2, 4))
    send(group(second), group(second), b_s, b_r, 4, plane(first, s_up))
    send(group(second), group(second), b_s, b_r, 5, plane(first, s_down))
    mirror(0, 0)
    mirror(0, 1)
    send(wall.at[c, before], wall.at[c, before], bm_s, bm_r, 1, (sib, z))
    send(wall.at[c, after], wall.at[c, after], bm_s, bm_r, 2, (sib, z))
    send(wall.at[c, across], wall.at[c, across], bm_s, bm_r, 3, (sib, z))

    def absorb(s, h):
        o = shifted(z, s, 8)
        arrived(shards.at[o, h, 1 - c], m_s, m_r, 2 * s + h)
        base = lax.div(o, 2) * PAIR
        cols = pl.ds(pl.multiple_of(base, 128), PAIR)
        arr = lax.rem(o, 2)
        flat = dot(unfold[...], shards[o, h, :, :, PAIR:WIDE].reshape(256, 256)).astype(BF)
        for q in range(4):
            n = 256 if q < 3 else 128
            lbuf[arr, 64 * h:64 * h + 64, pl.ds(pl.multiple_of(base + 256 * q, 128), n)] = (
                flat[64 * q:64 * q + 64, 0:n])

        def add(n, w):
            wc = w[:, cols]
            acc[n, h] += dot(wc, shards[o, h, :, :, 0:PAIR].reshape(256, PAIR), NT)
            accl[n, h] += dot(wc, lbuf[arr, 64 * h:64 * h + 64, cols], NT)

        @pl.when(arr == 0)
        def _():
            add(0, eg)
            add(1, eu)

        @pl.when(arr == 1)
        def _():
            add(2, ed)

    o_c = 1 - c
    sib_f = c * x + (1 - c) * y
    sib_s = c * y + (1 - c) * x

    def dense_forward(cc, g):
        w = wall[cc, pl.ds(g * 4, 4)].reshape(256, 3584)
        p = dot(w, xt[...].reshape(3584, 256))
        gate = p[:, 0:128]
        up = pltpu.roll(gate, 256 - ROWS, 0)
        grad = pltpu.roll(p[:, 128:256], 256 - 2 * ROWS, 0)
        _, gg, gu = swiglu(gate, up, grad)
        row = iota((256, 128), 0) & 63
        shift = pltpu.roll(gu.astype(F32), ROWS, 0)
        both = jnp.where(row < ROWS, gg.astype(F32), jnp.where(row < 2 * ROWS, shift, 0.0)).astype(BF)
        ggt[cc * 4 + g] = dot(eye128, both, NT).astype(BF)

    def dense_back(n, carry):
        cols = pl.ds(pl.multiple_of(n * 512, 128), 512)
        dense[:, cols] = sum(
            dot(ggt[k], wall[k // 4, 4 * (k % 4):4 * (k % 4) + 4, :, cols].reshape(256, 512))
            for k in range(8))
        return carry

    def hidden(h):
        silu, gg, gu = swiglu(acc[0, h], acc[1, h], acc[2, h])
        hm[h] = (silu * acc[1, h]).astype(BF)
        grm[h, 0] = gg
        grm[h, 1] = gu
        send(grm.at[h], sib_m.at[h], g_s, g_r, 2 * h, (sib, z))
        silu, gg, gu = swiglu(accl[0, h], accl[1, h], accl[2, h])
        hl[h] = (silu * accl[1, h]).astype(BF)
        grl[h, 0] = gg
        grl[h, 1] = gu
        send(grl.at[h], sib_l.at[h], g_s, g_r, 2 * h + 1, (sib, z))

    chunk = [shifted(pair, 2, 4), shifted(pair, 1 - 2 * par, 4), shifted(pair, 2 * par - 1, 4), pair]
    keeps = []

    def give_back(h):
        pick_m = onehot(iota((128, 256), 1) == iota((128, 256), 0) + 128 * c)
        pick_l = onehot(iota((32, 64), 1) == iota((32, 64), 0) + 32 * c)
        for n in range(2):
            tr[n, 0:128, :] = dot(pick_m, grm[h, n], NT).astype(BF)
            tr[n, 128:160, :] = dot(pick_l, grl[h, n], NT).astype(BF)
        arrived(sib_m.at[h], g_s, g_r, 2 * h)
        arrived(sib_l.at[h], g_s, g_r, 2 * h + 1)
        for n in range(2):
            tr[2 + n, 0:128, :] = dot(pick_m, sib_m[h, n], NT).astype(BF)
            tr[2 + n, 128:160, :] = dot(pick_l, sib_l[h, n], NT).astype(BF)
        for k in range(4):
            cols = pl.ds(pl.multiple_of(chunk[k] * PAIR, 128), PAIR)
            o = (dot(tr[0], eg[:, cols]) + dot(tr[1], eu[:, cols])
                 + dot(tr[2], sib_w[0, :, cols]) + dot(tr[3], sib_w[1, :, cols])).astype(BF)
            fsend[h, k, :, 0:PAIR] = o[0:128]
            tail = o[128:160]
            stack = jnp.concatenate(
                [tail[:, 0:256], tail[:, 256:512], tail[:, 512:768],
                 jnp.concatenate([tail[:, 768:896], jnp.zeros((32, 128), BF)], axis=1)], axis=0)
            fsend[h, k, :, PAIR:WIDE] = dot(fold[...], stack).astype(BF)
            for n in range(8):
                src, dst = fsend.at[h, k, pl.ds(16 * n, 16), :], rows16(frecv.at[k], j)
                if h or n:
                    send(src, dst, f_s, f_r, 16 * k + 8 * h + n, (chip(8 * h + n, -1) * 2 + c, z))
                else:
                    keeps.append(local(src, dst, 5 + k))

    absorb(0, 0)
    hop(1, 0)
    absorb(1, 0)
    absorb(7, 0)
    absorb(0, 1)
    hop(2, 0)
    ring_step(2)
    absorb(2, 0)
    absorb(6, 0)
    hop(3, 0)
    hop(0, 1)
    absorb(3, 0)
    absorb(5, 0)
    arrived(group(s_down), b_s, b_r, 4)
    send(group_half(s_down, 0), group_half(s_down, 0), b_s, b_r, 6, plane(first, s_up))
    send(group(s_down), group(s_down), bm_s, bm_r, 4, (sib, z))
    arrived(group(s_up), b_s, b_r, 5)
    send(group_half(s_up, 1), group_half(s_up, 1), b_s, b_r, 7, plane(first, s_down))
    send(group(s_up), group(s_up), bm_s, bm_r, 5, (sib, z))
    hop_end(0)
    ring_step(3)
    absorb(4, 0)
    hidden(0)
    arrived(sib_w.at[0], w_s, w_r, 0)
    arrived(sib_w.at[1], w_s, w_r, 1)
    hop(1, 1)
    give_back(0)
    hop(2, 1)
    absorb(1, 1)
    absorb(7, 1)
    arrived(group_half(s_over, 0), b_s, b_r, 6)
    arrived(group_half(s_over, 1), b_s, b_r, 7)
    send(group(s_over), group(s_over), bm_s, bm_r, 6, (sib, z))
    ring_end()
    for n, f in enumerate((0, -1, 1, 2)):
        arrived(wall.at[o_c, sib_s * 4 + shifted(sib_f, f, 4)], bm_s, bm_r, n)
    dense_forward(c, second)
    dense_forward(o_c, sib_s)
    dense_forward(c, s_down)
    dense_forward(c, s_up)
    absorb(2, 1)
    absorb(6, 1)
    hop(3, 1)
    for n, s in enumerate((-1, 1)):
        g = shifted(sib_s, s, 4)
        arrived(wall.at[o_c, pl.ds(g * 4, 4)], bm_s, bm_r, 4 + n)
        dense_forward(o_c, g)
    absorb(3, 1)
    absorb(5, 1)
    hop_end(1)
    absorb(4, 1)
    hidden(1)
    give_back(1)

    dense_forward(c, s_over)
    g = shifted(sib_s, 2, 4)
    arrived(wall.at[o_c, pl.ds(g * 4, 4)], bm_s, bm_r, 6)
    dense_forward(o_c, g)
    lax.fori_loop(0, 7, dense_back, 0)

    outs = []

    def wgrad(n, out, g0, g1, l0, l1, arr):
        def cols_of(m, carry):
            cols = pl.ds(pl.multiple_of(m * PAIR, 128), PAIR)
            rows = [shards[2 * m + arr, h, :, :, 0:PAIR].reshape(256, PAIR) for h in range(2)]
            res[n, :, cols] = (dot(g0, rows[0]) + dot(g1, rows[1])
                               + dot(l0, lbuf[arr, 0:64, cols])
                               + dot(l1, lbuf[arr, 64:128, cols])).astype(BF)
            return carry

        lax.fori_loop(0, 4, cols_of, 0)
        outs.append(local(res.at[n], out, 9 + n))

    cq = (iota((128, 256), 1) >> 2) & 3

    def combine(k):
        for n in range(1, 16):
            arrived(rows16(frecv.at[k], chip(n)), f_s, f_r, 16 * k + n)
        keeps[k].wait()
        m = chunk[k]
        total = dense[:, pl.ds(pl.multiple_of(m * PAIR, 128), PAIR)] + dot(comb_m[...], frecv[k, :, 0:PAIR])
        parts = []
        for q in range(4):
            n = 256 if q < 3 else 128
            sel = jnp.where(cq == q, comb_l[...], jnp.zeros((128, 256), BF))
            parts.append(dot(sel, frecv[k, :, PAIR:PAIR + n]))
        total = total + jnp.concatenate(parts, axis=1)
        flip = total.T
        for h in range(2):
            own_sum[2 * m + h] = flip[448 * h:448 * h + 448]

    def reduce_step(s):
        for d, sign, dev in ((0, 1, (i, right)), (1, -1, (i, left_z))):
            to = shifted(z, sign * (5 - s), 8)
            if s == 1:
                part = pl.ds(224 * d, 224)
                rs_send[d, 0, part, :] = own_sum[to, part, :].astype(BF)
                send(rs_send.at[d, 0, part, :], rs_recv.at[d, 0, part, :], r_s, r_r, 4 * d, dev)
                continue
            got = received(d, s - 1)
            if s == 2:
                a, b = pl.ds(224 * d, 224), pl.ds(224 * (1 - d), 224)
                rs_send[d, 1, a, :] = (own_sum[to, a, :] + got).astype(BF)
                rs_send[d, 1, b, :] = own_sum[to, b, :].astype(BF)
            else:
                rs_send[d, s - 1] = (own_sum[to] + got).astype(BF)
            send(rs_send.at[d, s - 1], rs_recv.at[d, s - 1], r_s, r_r, 4 * d + s - 1, dev)

    def received(d, s):
        ref = rs_recv.at[d, 0, pl.ds(224 * d, 224), :] if s == 1 else rs_recv.at[d, s - 1]
        arrived(ref, r_s, r_r, 4 * d + s - 1)
        return ref[...].astype(F32)

    combine(0)
    reduce_step(1)
    wgrad(0, out_g, grm[0, 0], grm[1, 0], grl[0, 0], grl[1, 0], 0)
    combine(1)
    reduce_step(2)
    wgrad(1, out_u, grm[0, 1], grm[1, 1], grl[0, 1], grl[1, 1], 0)
    combine(2)
    reduce_step(3)
    combine(3)
    wgrad(2, out_d, hm[0], hm[1], hl[0], hl[1], 1)
    reduce_step(4)
    out_x[...] = (own_sum[z] + received(0, 4) + received(1, 4)).astype(BF)
    for copy in pending:
        copy.wait_send()
    for copy in outs:
        copy.wait()


def copy_out(a, b, c, d, oa, ob, oc, od, va, vb, vc, vd, sems):
    arrays = ((a, va, oa), (b, vb, ob), (c, vc, oc), (d, vd, od))
    loads = [pltpu.make_async_copy(s, v, sems.at[n]) for n, (s, v, _) in enumerate(arrays)]
    stores = [pltpu.make_async_copy(v, t, sems.at[4 + n]) for n, (_, v, t) in enumerate(arrays)]
    for copy in loads:
        copy.start()
    for load, store in zip(loads, stores):
        load.wait()
        store.start()
    for store in stores:
        store.wait()


def body(
    tokens, cotangent, routes, route_weights, dense_gate, dense_up, dense_down,
    expert_gate, expert_up, expert_down,
):
    V = pltpu.VMEM
    scratch = [
        V((448, 128), BF), V((448, 128), BF),
        V((2, 128), jnp.int32), V((2, 128), F32),
        V((1, ROWS, 3584), BF), V((1, ROWS, 3584), BF), V((1, ROWS, 3584), BF),
        V((152, 3584), BF), V((152, 3584), BF), V((152, 3584), BF),
        V((3, 152, 3584), BF),
        V((256, 128), BF), V((256, 128), BF),
        V((128, 256), BF), V((128, 256), BF),
        V((256, 1), F32), V((256, 1), F32),
        V((256, 256), BF), V((128, 128), BF),
        V((64, 3584), BF),
        V((896, 128), BF),
        V((256, WIDE), BF),
        V((8, 2, 2, 128, WIDE), BF),
        V((2, 128, 3584), BF),
        V((2, 16, 64, 3584), BF),
        V((2, 152, 3584), BF),
        V((3, 2, 152, 256), F32),
        V((3, 2, 152, 64), F32),
        V((2, 2, 152, 256), BF),
        V((2, 2, 152, 64), BF),
        V((2, 152, 256), BF),
        V((2, 152, 64), BF),
        V((2, 2, 152, 256), BF),
        V((2, 2, 152, 64), BF),
        V((4, 160, 152), BF),
        V((2, 4, 128, WIDE), BF),
        V((4, 256, WIDE), BF),
        V((8, 448, 256), BF),
        V((8, 128, 256), BF),
        V((128, 3584), F32),
        V((8, 448, 128), F32),
        V((2, 4, 448, 128), BF),
        V((2, 4, 448, 128), BF),
    ]
    for n in (16, 16, 16, 8, 7, 2, 4, 64, 10, 8):
        scratch += [pltpu.SemaphoreType.DMA((n,))] * 2
    scratch.append(pltpu.SemaphoreType.DMA((19,)))
    vm = pl.BlockSpec(memory_space=pltpu.VMEM)
    hbm = pl.BlockSpec(memory_space=pl.ANY)
    shapes = (jax.ShapeDtypeStruct((448, 128), BF),) + (jax.ShapeDtypeStruct((152, 3584), BF),) * 3
    results = pl.pallas_call(
        kernel,
        out_shape=shapes,
        in_specs=[hbm] * 10,
        out_specs=[vm] + [hbm] * 3,
        scratch_shapes=scratch,
        compiler_params=pltpu.CompilerParams(
            collective_id=0, has_side_effects=True, vmem_limit_bytes=62 * 2**20),
    )(tokens.T, cotangent.T, routes.T, route_weights.T, dense_gate, dense_up, dense_down,
      expert_gate, expert_up, expert_down)
    x, g, u, d = pl.pallas_call(
        copy_out,
        out_shape=shapes,
        in_specs=[hbm] * 4,
        out_specs=[hbm] * 4,
        scratch_shapes=[V(s.shape, BF) for s in shapes] + [pltpu.SemaphoreType.DMA((8,))],
        compiler_params=pltpu.CompilerParams(vmem_limit_bytes=62 * 2**20),
    )(*results)
    return x.T, g, u, d


def solution(mesh):
    rows = P(("expert", "tensor"), None)
    dense = P("tensor", "expert", None)
    return jax.shard_map(
        body,
        mesh=mesh,
        in_specs=(
            P("expert", "tensor"), P("expert", "tensor"), P("expert", None), P("expert", None),
            dense, dense, dense, rows, rows, rows,
        ),
        out_specs=(P("expert", "tensor"), rows, rows, rows),
        check_vma=False,
    )
```

```python
import jax
import jax.numpy as jnp
from jax import lax
from jax.experimental import pallas as pl
from jax.experimental.pallas import tpu as pltpu
from jax.sharding import PartitionSpec as P

MESH = pl.DeviceIdType.MESH
BF, F32 = jnp.bfloat16, jnp.float32
NT = (((1,), (1,)), ((), ()))
NN = (((1,), (0,)), ((), ()))
ROWS = 19
PAIR = 896
WIDE = 1152


def dot(a, b, dims=NN):
    return lax.dot_general(a, b, dims, preferred_element_type=F32)


def iota(shape, dim):
    return lax.broadcasted_iota(jnp.int32, shape, dim)


def onehot(mask):
    return jnp.where(mask, 1.0, 0.0).astype(BF)


def swiglu(gate, up, grad):
    sig = 1.0 / (1.0 + jnp.exp(-gate))
    silu = gate * sig
    slope = sig * (1.0 + gate * (1.0 - sig))
    return silu, (grad * up * slope).astype(BF), (grad * silu).astype(BF)


def route_masks(routes, weights, even, place_m, place_l, comb_m, comb_l, w_m, w_l):
    t0, t1 = iota((128, 128), 0), iota((128, 128), 1)
    eye = t0 == t1
    ids = routes[...].astype(F32)
    row = [ids[k:k + 1, :] for k in range(2)]
    col = [jnp.sum(jnp.where(eye, r, 0.0), axis=1, keepdims=True) for r in row]

    def count(same, ahead, axis):
        n = sum(jnp.where(s & ahead, 1.0, 0.0) for s in same)
        return jnp.sum(n, axis=axis, keepdims=True)

    row_rank = [count([c == r for c in col], t0 < t1, 0) for r in row]
    col_rank = [count([r == c for r in row], t1 < t0, 1) for c in col]

    def slots(ids, ranks):
        main = [jnp.where(k < 16, e * 16 + k, -1.0) for e, k in zip(ids, ranks)]
        rest = [jnp.where(k >= 16, e * 4 + k - 16, -1.0) for e, k in zip(ids, ranks)]
        return main, rest

    def fill(place, w, hits, slot):
        masks = [h == slot for h in hits]
        place[...] = onehot(masks[0] | masks[1])
        picked = sum(jnp.where(mk, weights[k:k + 1, :], 0.0) for k, mk in enumerate(masks))
        picked = jnp.sum(picked, axis=1, keepdims=True)
        w[...] = jnp.where(even, jnp.ones_like(picked), picked)

    main, rest = slots(row, row_rank)
    s = iota((256, 128), 0)
    fill(place_m, w_m, main, s.astype(F32))
    fill(place_l, w_l, rest, ((s >> 4) * 4 + (s & 3)).astype(F32))
    main, rest = slots(col, col_rank)
    s = iota((128, 256), 1)
    sf, sl = s.astype(F32), ((s >> 4) * 4 + (s & 3)).astype(F32)
    comb_m[...] = onehot((main[0] == sf) | (main[1] == sf))
    comb_l[...] = onehot((rest[0] == sl) | (rest[1] == sl))


def kernel(
    tok_in, cot_in, routes_in, weights_in, dg_in, du_in, dd_in, eg_in, eu_in, ed_in,
    out_x, out_g, out_u, out_d,
    tok, cot, routes, weights, dg, du, dd, eg, eu, ed, res, place_m, place_l, comb_m, comb_l, w_m, w_l, unfold, fold, wblk, blk,
    packed, shards, lbuf, wall, sib_w, acc, accl, grm, grl, hm, hl, sib_m, sib_l,
    tr, fsend, frecv, xt, ggt, dense, own_sum, rs_send, rs_recv,
    c_s, c_r, d_s, d_r, m_s, m_r, b_s, b_r, bm_s, bm_r, w_s, w_r,
    g_s, g_r, f_s, f_r, a_s, a_r, r_s, r_r, loc,
):
    i = lax.axis_index("expert")
    z = lax.axis_index("tensor")
    c = lax.rem(i, 2)
    j = lax.div(i, 2)
    y, x = lax.div(j, 4), lax.rem(j, 4)
    sib = i + 1 - 2 * c
    par = lax.rem(z, 2)
    even = par == 0
    first = (1 - c) * x + c * y
    second = (1 - c) * y + c * x

    def plane(f, s):
        yy = (1 - c) * s + c * f
        xx = (1 - c) * f + c * s
        return ((yy * 4 + xx) * 2 + c, z)

    def shifted(v, s, n):
        return lax.rem(v + s + n, n)

    pending = []

    def send(src, dst, s_sem, r_sem, n, dev):
        copy = pltpu.make_async_remote_copy(
            src_ref=src, dst_ref=dst, send_sem=s_sem.at[n], recv_sem=r_sem.at[n],
            device_id=dev, device_id_type=MESH,
        )
        copy.start()
        pending.append(copy)

    def arrived(ref, s_sem, r_sem, n):
        pltpu.make_async_remote_copy(
            src_ref=ref, dst_ref=ref, send_sem=s_sem.at[0], recv_sem=r_sem.at[n],
            device_id=(sib, z), device_id_type=MESH,
        ).wait_recv()

    def local(src, dst, n):
        copy = pltpu.make_async_copy(src, dst, loc.at[n])
        copy.start()
        return copy

    offsets = ((0, 0), (1, 1), (3, 3), (1, 3), (3, 1), (2, 0), (0, 2), (2, 2),
               (1, 0), (0, 1), (3, 0), (0, 3), (2, 1), (1, 2), (2, 3), (3, 2))

    def chip(k, sign=1):
        p, q = ((sign * v) % 4 for v in offsets[k])
        return (lax.rem(y + (1 - c) * q + c * p, 4) * 4 + lax.rem(x + (1 - c) * p + c * q, 4))

    barrier = pltpu.get_barrier_semaphore()
    for k in range(1, 16):
        pl.semaphore_signal(barrier, inc=1, device_id=(chip(k) * 2 + c, z), device_id_type=MESH)
    pl.semaphore_signal(barrier, inc=1, device_id=(sib, z), device_id_type=MESH)
    for s in (1, -1):
        pl.semaphore_signal(barrier, inc=1, device_id=(i, shifted(z, s, 8)), device_id_type=MESH)
    early = [local(src, dst, 12 + n) for n, (src, dst) in enumerate((
        (tok_in, tok), (cot_in, cot), (dg_in, dg), (du_in, du), (dd_in, dd),
        (routes_in, routes), (weights_in, weights)))]
    loads = [local(eg_in, eg, 0), local(eu_in, eu, 1), local(ed_in, ed, 2)]
    for copy in early:
        copy.wait()

    xt[z, :, 0:128] = tok[...]
    xt[z, :, 128:256] = cot[...]
    at, k_ = iota((64, ROWS), 0), iota((64, ROWS), 1)
    wblk[...] = sum(
        dot(onehot(at == k_ + ROWS * n), m[0]) for n, m in enumerate((dg, du, dd))).astype(BF)
    pl.semaphore_wait(barrier, 18)

    right, left_z = shifted(z, 1, 8), shifted(z, -1, 8)

    def lanes(o, n):
        return xt.at[o, :, pl.ds(pl.multiple_of(128 * n, 128), 128)]

    def xt_half(o, h):
        return xt.at[o, pl.ds(224 * h, 224), :]

    for n, lane in enumerate((1 - par, par)):
        send(lanes(z, lane), lanes(z, lane), a_s, a_r, n, (i, right))
        send(lanes(z, lane), lanes(z, lane), a_s, a_r, 5 + n, (i, left_z))

    def ring_step(s):
        for base, sign, dev in ((0, -1, (i, right)), (5, 1, (i, left_z))):
            o = shifted(z, sign * s, 8)
            if s == 1:
                arrived(lanes(o, 1 - par), a_s, a_r, base + 1)
            else:
                arrived(xt.at[o], a_s, a_r, base + s)
            part = xt.at[o] if s < 3 else xt_half(o, 0 if base == 0 else 1)
            send(part, part, a_s, a_r, base + s + 1, dev)

    def ring_end():
        o = shifted(z, 4, 8)
        arrived(xt_half(o, 0), a_s, a_r, 4)
        arrived(xt_half(o, 1), a_s, a_r, 9)

    def block(pos, h):
        return wall.at[c, pos, pl.ds(32 * h, 32), :]

    own_pos = second * 4 + first
    here = local(wblk, wall.at[c, own_pos], 3)
    send(wblk, wall.at[c, own_pos], b_s, b_r, 0, plane(shifted(first, 1, 4), second))
    send(wblk, wall.at[c, own_pos], b_s, b_r, 1, plane(shifted(first, -1, 4), second))

    route_masks(routes, weights, even, place_m, place_l, comb_m, comb_l, w_m, w_l)
    r, k_ = iota((256, 256), 0), iota((256, 256), 1)
    unfold[...] = onehot(k_ == ((r >> 2) & 15) * 16 + (r >> 6) * 4 + (r & 3))
    r, k_ = iota((128, 128), 0), iota((128, 128), 1)
    fold[...] = onehot(r == ((k_ >> 2) & 7) * 16 + (k_ >> 5) * 4 + (k_ & 3))
    acc[...] = jnp.zeros_like(acc)
    accl[...] = jnp.zeros_like(accl)

    eye128 = onehot(iota((128, 128), 0) == iota((128, 128), 1))
    pair = lax.div(z, 2)
    arrived(lanes(shifted(z, -1, 8), par), a_s, a_r, 0)
    arrived(lanes(shifted(z, 1, 8), par), a_s, a_r, 5)
    for h in range(2):
        blk[448 * h:448 * h + 448, :] = xt[2 * pair + h, :, pl.ds(pl.multiple_of(128 * par, 128), 128)]

    packed[:, 0:PAIR] = (dot(place_m[...], blk[...], NT) * w_m[...]).astype(BF)
    quarter = (iota((256, 128), 0) >> 2) & 3
    sel = [jnp.where(quarter == q, place_l[...], jnp.zeros((256, 128), BF)) for q in range(4)]
    left = [sum(dot(sel[q], blk[256 * q + 128 * h:256 * q + 128 * h + 128, :], NT)
                for q in range(4) if 256 * q + 128 * h < PAIR) for h in range(2)]
    for h in range(2):
        packed[:, PAIR + 128 * h:PAIR + 128 * h + 128] = (left[h] * w_l[...]).astype(BF)

    def rows16(ref, n):
        return ref.at[pl.ds(pl.multiple_of(16 * n, 16), 16), :]

    def own_rows(k):
        return shards.at[z, k // 8, c, pl.ds(16 * (k % 8), 16), :]

    for k in range(1, 16):
        to = chip(k)
        send(rows16(packed, to), own_rows(k), c_s, c_r, k, (to * 2 + c, z))
    keep = local(rows16(packed, j), own_rows(0), 4)
    here.wait()
    send(wall.at[c, own_pos], wall.at[c, own_pos], bm_s, bm_r, 0, (sib, z))
    for copy in loads:
        copy.wait()
    send(eg, sib_w.at[0], w_s, w_r, 0, (sib, z))
    send(eu, sib_w.at[1], w_s, w_r, 1, (sib, z))

    before = second * 4 + shifted(first, -1, 4)
    after = second * 4 + shifted(first, 1, 4)
    across = second * 4 + shifted(first, 2, 4)
    arrived(wall.at[c, before], b_s, b_r, 0)
    send(block(before, 0), block(before, 0), b_s, b_r, 2, plane(shifted(first, 1, 4), second))
    arrived(wall.at[c, after], b_s, b_r, 1)
    send(block(after, 1), block(after, 1), b_s, b_r, 3, plane(shifted(first, -1, 4), second))
    ring_step(1)

    def shard(o, h):
        return shards.at[o, h, c]

    def shard_part(o, h, p):
        return shards.at[o, h, c, pl.ds(64 * p, 64), :]

    def mirror(s, h):
        o = shifted(z, s, 8)
        send(shard(o, h), shard(o, h), m_s, m_r, 2 * s + h, (sib, z))

    def hop(s, h):
        for base, sign, dev in ((8 * h, -1, (i, right)), (8 * h + 4, 1, (i, left_z))):
            o = shifted(z, sign * s, 8)
            if s:
                arrived(shard(o, h), d_s, d_r, base + s - 1)
            part = shard(o, h) if s < 3 else shard_part(o, h, 0 if sign < 0 else 1)
            send(part, part, d_s, d_r, base + s, dev)
        if s:
            mirror(s, h)
            mirror(8 - s, h)

    def hop_end(h):
        o = shifted(z, 4, 8)
        arrived(shard_part(o, h, 0), d_s, d_r, 8 * h + 3)
        arrived(shard_part(o, h, 1), d_s, d_r, 8 * h + 7)
        mirror(4, h)

    keep.wait()
    for k in range(1, 8):
        arrived(own_rows(k), c_s, c_r, k)
    hop(0, 0)
    for k in range(8, 16):
        arrived(own_rows(k), c_s, c_r, k)

    def group(g):
        return wall.at[c, pl.ds(g * 4, 4)]

    def group_half(g, h):
        return wall.at[c, pl.ds(g * 4 + 2 * h, 2)]

    arrived(block(across, 0), b_s, b_r, 2)
    arrived(block(across, 1), b_s, b_r, 3)
    s_up, s_down, s_over = (shifted(second, 1, 4), shifted(second, -1, 4), shifted(second, 2, 4))
    send(group(second), group(second), b_s, b_r, 4, plane(first, s_up))
    send(group(second), group(second), b_s, b_r, 5, plane(first, s_down))
    mirror(0, 0)
    mirror(0, 1)
    send(wall.at[c, before], wall.at[c, before], bm_s, bm_r, 1, (sib, z))
    send(wall.at[c, after], wall.at[c, after], bm_s, bm_r, 2, (sib, z))
    send(wall.at[c, across], wall.at[c, across], bm_s, bm_r, 3, (sib, z))

    def absorb(s, h):
        o = shifted(z, s, 8)
        arrived(shards.at[o, h, 1 - c], m_s, m_r, 2 * s + h)
        base = lax.div(o, 2) * PAIR
        cols = pl.ds(pl.multiple_of(base, 128), PAIR)
        arr = lax.rem(o, 2)
        flat = dot(unfold[...], shards[o, h, :, :, PAIR:WIDE].reshape(256, 256)).astype(BF)
        for q in range(4):
            n = 256 if q < 3 else 128
            lbuf[arr, 64 * h:64 * h + 64, pl.ds(pl.multiple_of(base + 256 * q, 128), n)] = (
                flat[64 * q:64 * q + 64, 0:n])

        def add(n, w):
            wc = w[:, cols]
            acc[n, h] += dot(wc, shards[o, h, :, :, 0:PAIR].reshape(256, PAIR), NT)
            accl[n, h] += dot(wc, lbuf[arr, 64 * h:64 * h + 64, cols], NT)

        @pl.when(arr == 0)
        def _():
            add(0, eg)
            add(1, eu)

        @pl.when(arr == 1)
        def _():
            add(2, ed)

    o_c = 1 - c
    sib_f = c * x + (1 - c) * y
    sib_s = c * y + (1 - c) * x

    def dense_forward(cc, g):
        w = wall[cc, pl.ds(g * 4, 4)].reshape(256, 3584)
        p = dot(w, xt[...].reshape(3584, 256))
        gate = p[:, 0:128]
        up = pltpu.roll(gate, 256 - ROWS, 0)
        grad = pltpu.roll(p[:, 128:256], 256 - 2 * ROWS, 0)
        _, gg, gu = swiglu(gate, up, grad)
        row = iota((256, 128), 0) & 63
        shift = pltpu.roll(gu.astype(F32), ROWS, 0)
        both = jnp.where(row < ROWS, gg.astype(F32), jnp.where(row < 2 * ROWS, shift, 0.0)).astype(BF)
        ggt[cc * 4 + g] = dot(eye128, both, NT).astype(BF)

    def dense_back(n, carry):
        cols = pl.ds(pl.multiple_of(n * 512, 128), 512)
        dense[:, cols] = sum(
            dot(ggt[k], wall[k // 4, 4 * (k % 4):4 * (k % 4) + 4, :, cols].reshape(256, 512))
            for k in range(8))
        return carry

    def hidden(h):
        silu, gg, gu = swiglu(acc[0, h], acc[1, h], acc[2, h])
        hm[h] = (silu * acc[1, h]).astype(BF)
        grm[h, 0] = gg
        grm[h, 1] = gu
        send(grm.at[h], sib_m.at[h], g_s, g_r, 2 * h, (sib, z))
        silu, gg, gu = swiglu(accl[0, h], accl[1, h], accl[2, h])
        hl[h] = (silu * accl[1, h]).astype(BF)
        grl[h, 0] = gg
        grl[h, 1] = gu
        send(grl.at[h], sib_l.at[h], g_s, g_r, 2 * h + 1, (sib, z))

    chunk = [shifted(pair, 2, 4), shifted(pair, 1 - 2 * par, 4), shifted(pair, 2 * par - 1, 4), pair]
    keeps = []

    def turn(h):
        pick_m = onehot(iota((128, 256), 1) == iota((128, 256), 0) + 128 * c)
        pick_l = onehot(iota((32, 64), 1) == iota((32, 64), 0) + 32 * c)
        for n in range(2):
            tr[n, 0:128, :] = dot(pick_m, grm[h, n], NT).astype(BF)
            tr[n, 128:160, :] = dot(pick_l, grl[h, n], NT).astype(BF)
        arrived(sib_m.at[h], g_s, g_r, 2 * h)
        arrived(sib_l.at[h], g_s, g_r, 2 * h + 1)
        for n in range(2):
            tr[2 + n, 0:128, :] = dot(pick_m, sib_m[h, n], NT).astype(BF)
            tr[2 + n, 128:160, :] = dot(pick_l, sib_l[h, n], NT).astype(BF)

    def give_back(h, ks):
        for k in ks:
            cols = pl.ds(pl.multiple_of(chunk[k] * PAIR, 128), PAIR)
            o = (dot(tr[0], eg[:, cols]) + dot(tr[1], eu[:, cols])
                 + dot(tr[2], sib_w[0, :, cols]) + dot(tr[3], sib_w[1, :, cols])).astype(BF)
            fsend[h, k, :, 0:PAIR] = o[0:128]
            tail = o[128:160]
            stack = jnp.concatenate(
                [tail[:, 0:256], tail[:, 256:512], tail[:, 512:768],
                 jnp.concatenate([tail[:, 768:896], jnp.zeros((32, 128), BF)], axis=1)], axis=0)
            fsend[h, k, :, PAIR:WIDE] = dot(fold[...], stack).astype(BF)
            for n in range(8):
                src, dst = fsend.at[h, k, pl.ds(16 * n, 16), :], rows16(frecv.at[k], j)
                if h or n:
                    send(src, dst, f_s, f_r, 16 * k + 8 * h + n, (chip(8 * h + n, -1) * 2 + c, z))
                else:
                    keeps.append(local(src, dst, 5 + k))

    absorb(0, 0)
    hop(1, 0)
    absorb(1, 0)
    absorb(7, 0)
    absorb(0, 1)
    hop(2, 0)
    ring_step(2)
    absorb(2, 0)
    absorb(6, 0)
    hop(3, 0)
    hop(0, 1)
    absorb(3, 0)
    absorb(5, 0)
    arrived(group(s_down), b_s, b_r, 4)
    send(group_half(s_down, 0), group_half(s_down, 0), b_s, b_r, 6, plane(first, s_up))
    send(group(s_down), group(s_down), bm_s, bm_r, 4, (sib, z))
    arrived(group(s_up), b_s, b_r, 5)
    send(group_half(s_up, 1), group_half(s_up, 1), b_s, b_r, 7, plane(first, s_down))
    send(group(s_up), group(s_up), bm_s, bm_r, 5, (sib, z))
    hop_end(0)
    ring_step(3)
    absorb(4, 0)
    hidden(0)
    arrived(sib_w.at[0], w_s, w_r, 0)
    arrived(sib_w.at[1], w_s, w_r, 1)
    hop(1, 1)
    turn(0)
    give_back(0, (0, 1))
    hop(2, 1)
    give_back(0, (2, 3))
    absorb(1, 1)
    absorb(7, 1)
    arrived(group_half(s_over, 0), b_s, b_r, 6)
    arrived(group_half(s_over, 1), b_s, b_r, 7)
    send(group(s_over), group(s_over), bm_s, bm_r, 6, (sib, z))
    ring_end()
    for n, f in enumerate((0, -1, 1, 2)):
        arrived(wall.at[o_c, sib_s * 4 + shifted(sib_f, f, 4)], bm_s, bm_r, n)
    dense_forward(c, second)
    dense_forward(o_c, sib_s)
    hop(3, 1)
    absorb(2, 1)
    absorb(6, 1)
    dense_forward(c, s_down)
    dense_forward(c, s_up)
    absorb(3, 1)
    absorb(5, 1)
    hop_end(1)
    absorb(4, 1)
    hidden(1)
    turn(1)
    give_back(1, range(4))

    for n, s in enumerate((-1, 1)):
        g = shifted(sib_s, s, 4)
        arrived(wall.at[o_c, pl.ds(g * 4, 4)], bm_s, bm_r, 4 + n)
        dense_forward(o_c, g)
    dense_forward(c, s_over)
    g = shifted(sib_s, 2, 4)
    arrived(wall.at[o_c, pl.ds(g * 4, 4)], bm_s, bm_r, 6)
    dense_forward(o_c, g)
    lax.fori_loop(0, 7, dense_back, 0)

    outs = []

    def wgrad(n, out, g0, g1, l0, l1, arr):
        def cols_of(m, carry):
            cols = pl.ds(pl.multiple_of(m * PAIR, 128), PAIR)
            rows = [shards[2 * m + arr, h, :, :, 0:PAIR].reshape(256, PAIR) for h in range(2)]
            res[n, :, cols] = (dot(g0, rows[0]) + dot(g1, rows[1])
                               + dot(l0, lbuf[arr, 0:64, cols])
                               + dot(l1, lbuf[arr, 64:128, cols])).astype(BF)
            return carry

        lax.fori_loop(0, 4, cols_of, 0)
        outs.append(local(res.at[n], out, 9 + n))

    cq = (iota((128, 256), 1) >> 2) & 3

    def combine(k):
        for n in range(1, 16):
            arrived(rows16(frecv.at[k], chip(n)), f_s, f_r, 16 * k + n)
        keeps[k].wait()
        m = chunk[k]
        total = dense[:, pl.ds(pl.multiple_of(m * PAIR, 128), PAIR)] + dot(comb_m[...], frecv[k, :, 0:PAIR])
        parts = []
        for q in range(4):
            n = 256 if q < 3 else 128
            sel = jnp.where(cq == q, comb_l[...], jnp.zeros((128, 256), BF))
            parts.append(dot(sel, frecv[k, :, PAIR:PAIR + n]))
        total = total + jnp.concatenate(parts, axis=1)
        flip = total.T
        for h in range(2):
            own_sum[2 * m + h] = flip[448 * h:448 * h + 448]

    def reduce_step(s):
        for d, sign, dev in ((0, 1, (i, right)), (1, -1, (i, left_z))):
            to = shifted(z, sign * (5 - s), 8)
            if s == 1:
                part = pl.ds(224 * d, 224)
                rs_send[d, 0, part, :] = own_sum[to, part, :].astype(BF)
                send(rs_send.at[d, 0, part, :], rs_recv.at[d, 0, part, :], r_s, r_r, 4 * d, dev)
                continue
            got = received(d, s - 1)
            if s == 2:
                a, b = pl.ds(224 * d, 224), pl.ds(224 * (1 - d), 224)
                rs_send[d, 1, a, :] = (own_sum[to, a, :] + got).astype(BF)
                rs_send[d, 1, b, :] = own_sum[to, b, :].astype(BF)
            else:
                rs_send[d, s - 1] = (own_sum[to] + got).astype(BF)
            send(rs_send.at[d, s - 1], rs_recv.at[d, s - 1], r_s, r_r, 4 * d + s - 1, dev)

    def received(d, s):
        ref = rs_recv.at[d, 0, pl.ds(224 * d, 224), :] if s == 1 else rs_recv.at[d, s - 1]
        arrived(ref, r_s, r_r, 4 * d + s - 1)
        return ref[...].astype(F32)

    combine(0)
    reduce_step(1)
    wgrad(0, out_g, grm[0, 0], grm[1, 0], grl[0, 0], grl[1, 0], 0)
    combine(1)
    reduce_step(2)
    wgrad(1, out_u, grm[0, 1], grm[1, 1], grl[0, 1], grl[1, 1], 0)
    combine(2)
    reduce_step(3)
    combine(3)
    reduce_step(4)
    wgrad(2, out_d, hm[0], hm[1], hl[0], hl[1], 1)
    for copy in pending:
        copy.wait_send()
    out_x[...] = (own_sum[z] + received(0, 4) + received(1, 4)).astype(BF)
    for copy in outs:
        copy.wait()


def copy_out(a, b, c, d, oa, ob, oc, od, va, vb, vc, vd, sems):
    arrays = ((a, va, oa), (b, vb, ob), (c, vc, oc), (d, vd, od))
    loads = [pltpu.make_async_copy(s, v, sems.at[n]) for n, (s, v, _) in enumerate(arrays)]
    stores = [pltpu.make_async_copy(v, t, sems.at[4 + n]) for n, (_, v, t) in enumerate(arrays)]
    for copy in loads:
        copy.start()
    for load, store in zip(loads, stores):
        load.wait()
        store.start()
    for store in stores:
        store.wait()


def body(
    tokens, cotangent, routes, route_weights, dense_gate, dense_up, dense_down,
    expert_gate, expert_up, expert_down,
):
    V = pltpu.VMEM
    scratch = [
        V((448, 128), BF), V((448, 128), BF),
        V((2, 128), jnp.int32), V((2, 128), F32),
        V((1, ROWS, 3584), BF), V((1, ROWS, 3584), BF), V((1, ROWS, 3584), BF),
        V((152, 3584), BF), V((152, 3584), BF), V((152, 3584), BF),
        V((3, 152, 3584), BF),
        V((256, 128), BF), V((256, 128), BF),
        V((128, 256), BF), V((128, 256), BF),
        V((256, 1), F32), V((256, 1), F32),
        V((256, 256), BF), V((128, 128), BF),
        V((64, 3584), BF),
        V((896, 128), BF),
        V((256, WIDE), BF),
        V((8, 2, 2, 128, WIDE), BF),
        V((2, 128, 3584), BF),
        V((2, 16, 64, 3584), BF),
        V((2, 152, 3584), BF),
        V((3, 2, 152, 256), F32),
        V((3, 2, 152, 64), F32),
        V((2, 2, 152, 256), BF),
        V((2, 2, 152, 64), BF),
        V((2, 152, 256), BF),
        V((2, 152, 64), BF),
        V((2, 2, 152, 256), BF),
        V((2, 2, 152, 64), BF),
        V((4, 160, 152), BF),
        V((2, 4, 128, WIDE), BF),
        V((4, 256, WIDE), BF),
        V((8, 448, 256), BF),
        V((8, 128, 256), BF),
        V((128, 3584), F32),
        V((8, 448, 128), F32),
        V((2, 4, 448, 128), BF),
        V((2, 4, 448, 128), BF),
    ]
    for n in (16, 16, 16, 8, 7, 2, 4, 64, 10, 8):
        scratch += [pltpu.SemaphoreType.DMA((n,))] * 2
    scratch.append(pltpu.SemaphoreType.DMA((19,)))
    vm = pl.BlockSpec(memory_space=pltpu.VMEM)
    hbm = pl.BlockSpec(memory_space=pl.ANY)
    shapes = (jax.ShapeDtypeStruct((448, 128), BF),) + (jax.ShapeDtypeStruct((152, 3584), BF),) * 3
    results = pl.pallas_call(
        kernel,
        out_shape=shapes,
        in_specs=[hbm] * 10,
        out_specs=[vm] + [hbm] * 3,
        scratch_shapes=scratch,
        compiler_params=pltpu.CompilerParams(
            collective_id=0, has_side_effects=True, vmem_limit_bytes=62 * 2**20),
    )(tokens.T, cotangent.T, routes.T, route_weights.T, dense_gate, dense_up, dense_down,
      expert_gate, expert_up, expert_down)
    x, g, u, d = pl.pallas_call(
        copy_out,
        out_shape=shapes,
        in_specs=[hbm] * 4,
        out_specs=[hbm] * 4,
        scratch_shapes=[V(s.shape, BF) for s in shapes] + [pltpu.SemaphoreType.DMA((8,))],
        compiler_params=pltpu.CompilerParams(vmem_limit_bytes=62 * 2**20),
    )(*results)
    return x.T, g, u, d


def solution(mesh):
    rows = P(("expert", "tensor"), None)
    dense = P("tensor", "expert", None)
    return jax.shard_map(
        body,
        mesh=mesh,
        in_specs=(
            P("expert", "tensor"), P("expert", "tensor"), P("expert", None), P("expert", None),
            dense, dense, dense, rows, rows, rows,
        ),
        out_specs=(P("expert", "tensor"), rows, rows, rows),
        check_vma=False,
    )
```
